128 devices in a mesh: seq: 32 (over x, y, core), head: 4 (over z).
Axes of the slice: x: 4, y: 4, z: 4, core: 2. Of those that a mesh axis runs over, the one named last changes fastest.
Arguments:
- queries: bfloat16 [8192, 2048], P('seq', 'head'), may hold values from -6 to 6
- keys: bfloat16 [8192, 2048], P('seq', 'head'), may hold values from -4 to 4
- values: bfloat16 [8192, 2048], P('seq', 'head'), may hold values from -4 to 4
- rates: float32 [8192, 32], P('seq', 'head'), may hold values from 0 to 0.004938272
- start_state: float32 [32, 64, 65], P('head'), may hold values from -2 to 2
- out_weight: bfloat16 [2048, 2048], P('head'), may hold values from -0.125 to 0.125
Outputs:
- mixed: bfloat16 [8192, 2048], P(('seq', 'head'))
The draws below stay inside these ranges and needn't reach their ends.
All inputs are finite; a program needn't handle non-finite values.
Results may differ from the reference program's by a relative error of at most 0.015.
Values may be sent and summed in bfloat16 or wider, within the bound.
A program may use at most 192 MiB of HBM per device.

```python
import math
import jax
import jax.numpy as jnp
from jax import lax

D = 2048
H = 32
HD = 64
MINIBATCH_TOKENS = 16
TOK_DEV = 256
TOKENS = 8192


def shared_keys(key):
    normal_part = jax.random.normal(jax.random.fold_in(key, 11), (TOKENS, H * HD), jnp.float32)
    return jnp.clip(normal_part, -4.0, 4.0)


def draw_keys(key, part):
    scaled = shared_keys(key)
    return scaled.astype(jnp.bfloat16)


def draw_values(key, part):
    scaled = shared_keys(key)
    key = jax.random.fold_in(key, 5)
    shaped = scaled.reshape(TOKENS, H, HD)
    direct = jax.random.uniform(jax.random.fold_in(key, 1), (H, HD), jnp.float32, -1.2, 1.2)
    across = jax.random.uniform(jax.random.fold_in(key, 2), (H, HD), jnp.float32, -0.8, 0.8)
    noise = jax.random.normal(jax.random.fold_in(key, 3), (TOKENS, H, HD), jnp.float32)
    blended = direct * shaped + across * jnp.roll(shaped, 1, axis=2) + 0.5 * noise
    return jnp.clip(blended, -4.0, 4.0).reshape(TOKENS, H * HD).astype(jnp.bfloat16)


def draw_rates(key, part):
    key = jax.random.fold_in(key, 7)
    upper_limit = 0.4 / (MINIBATCH_TOKENS + HD + 1)
    floor_rate = 0.5 / TOKENS
    top_rate = upper_limit
    head_log = jax.random.uniform(jax.random.fold_in(key, 1), (H,), jnp.float32, math.log(floor_rate), math.log(top_rate))
    shard_log = jax.random.uniform(jax.random.fold_in(key, 2), (TOKENS // TOK_DEV, H), jnp.float32, -0.69, 0.0)
    token_wise = jnp.exp(head_log[None, :] + jnp.repeat(shard_log, TOK_DEV, axis=0))
    count_of_blocks = TOKENS // MINIBATCH_TOKENS
    probability = jax.random.uniform(jax.random.fold_in(key, 3), (count_of_blocks, H), jnp.float32) < 4.0 / count_of_blocks
    mandatory = jax.random.randint(jax.random.fold_in(key, 4), (H,), 0, count_of_blocks)
    token_spurts = jnp.logical_or(probability, jnp.arange(count_of_blocks)[:, None] == mandatory[None, :])
    spurt_tokens = jnp.repeat(token_spurts, MINIBATCH_TOKENS, axis=0)
    return jnp.where(spurt_tokens, upper_limit, jnp.minimum(token_wise, upper_limit)).astype(jnp.float32)


def levels(key, extent, shards, least, high):
    def one(position, blocks):
        heights = jax.random.uniform(jax.random.fold_in(jax.random.fold_in(key, 6), position), (blocks,), jnp.float32, least / len(shards), high / len(shards))
        return jnp.repeat(jnp.exp(heights), extent[position] // blocks).reshape((-1,) + (1,) * (len(extent) - position - 1))

    gain = one(*shards[0])
    for cut in shards[1:]:
        gain = gain * one(*cut)
    return gain


def scatter_about(rng, dims, scale, most, split=(), kind=jnp.bfloat16):
    entries = scale * jax.random.normal(rng, dims, jnp.float32)
    if split:
        entries = entries * levels(rng, dims, split, -0.22, 0.18)
    return jnp.clip(entries, -most, most).astype(kind)


def setup_inputs(seed: int = 0) -> dict:
    seeds = jax.random.split(jax.random.key(seed), 7)
    return {
        "queries": scatter_about(seeds[0], (TOKENS, H * HD), 1.0, 6.0, ((0, 32), (1, 4))),
        "keys": draw_keys(jax.random.fold_in(seeds[6], 71), 0),
        "values": draw_values(jax.random.fold_in(seeds[6], 71), 0),
        "rates": draw_rates(jax.random.fold_in(seeds[6], 71), 0),
        "start_state": scatter_about(seeds[4], (H, HD, HD + 1), 0.125, 2.0, ((0, 4),), jnp.float32),
        "out_weight": scatter_about(seeds[5], (H * HD, D), (H * HD) ** -0.5, 0.125, ((0, 4),)),
    }


highest = lax.Precision.HIGHEST


def with_one(source):
    return jnp.concatenate([source, jnp.ones(source.shape[:-1] + (1,), jnp.float32)], axis=-1)


def reference(queries, keys, values, rates, start_state, out_weight):
    blocks = TOKENS // MINIBATCH_TOKENS

    def heads_view(source):
        return source.reshape(blocks, MINIBATCH_TOKENS, H, HD).transpose(0, 2, 1, 3)

    causal = (jnp.arange(MINIBATCH_TOKENS)[:, None] >= jnp.arange(MINIBATCH_TOKENS)[None, :]).astype(jnp.float32)

    def update(inner_state, inputs):
        query_blk, key_blk, value_blk, rate_blk = inputs
        query_hat = with_one(query_blk.astype(jnp.float32))
        key_hat = with_one(key_blk.astype(jnp.float32))
        target = value_blk.astype(jnp.float32)
        residue = jnp.einsum('hdb,hsb->hsd', inner_state, key_hat, precision=highest) - target
        seen_weight = jnp.einsum('htb,hsb->hts', query_hat, key_hat, precision=highest) * causal[None] * rate_blk[:, None, :]
        result = jnp.einsum('hdb,htb->htd', inner_state, query_hat, precision=highest) - jnp.einsum('hts,hsd->htd', seen_weight, residue, precision=highest)
        gradient = jnp.einsum('hsd,hsb->hdb', residue * rate_blk[:, :, None], key_hat, precision=highest)
        return inner_state - gradient, result

    step_rate = rates.astype(jnp.float32).reshape(blocks, MINIBATCH_TOKENS, H).transpose(0, 2, 1)
    last_state, results = lax.scan(update, start_state.astype(jnp.float32), (heads_view(queries), heads_view(keys), heads_view(values), step_rate))
    ttt_out = results.transpose(0, 2, 1, 3).reshape(TOKENS, H * HD).astype(jnp.bfloat16)
    return jnp.dot(ttt_out, out_weight, preferred_element_type=jnp.float32).astype(jnp.bfloat16)
```

```python
import jax
import jax.numpy as jnp
from jax import lax
from jax.experimental import pallas as pl
from jax.experimental.pallas import tpu as pltpu
from jax.sharding import PartitionSpec as P

HD = 64
MINIBATCH_TOKENS = 16
TOK = 256
HALF = TOK // 2
PAIRS = 4
GROUP = 8
GROUPS = 4
RING = 4
FEAT = 80
LANES = 128
WIDTH = 2048
ROWS = TOK // RING
MESH = pl.DeviceIdType.MESH
F32 = jnp.float32
BF16 = jnp.bfloat16


def dot(left, right):
    return jnp.dot(left, right, preferred_element_type=F32)


def kernel(
    q_hbm, k_hbm, v_hbm, rate_ref, start_hbm, w_hbm, out_ref,
    q_ref, k_ref, v_ref, w_ref, start_ref,
    u_ref, kt_ref, qt_ref, py_ref,
    send1, recv1, prefix, send2, recv2, state, send3, recv3,
    far_send, far_recv, near_send, near_recv,
    load_sem, send_sem1, recv_sem1, send_sem2, recv_sem2, send_sem3, recv_sem3,
    far_send_sem, far_recv_sem, near_send_sem, near_recv_sem,
):
    seq = lax.axis_index("seq")
    head = lax.axis_index("head")
    group = seq // GROUP
    place = lax.rem(seq, GROUP)
    chip = place // 2
    core = lax.rem(place, 2)
    base = group * GROUP

    loads = [
        pltpu.make_async_copy(k_hbm, k_ref, load_sem.at[0]),
        pltpu.make_async_copy(v_hbm, v_ref, load_sem.at[1]),
        pltpu.make_async_copy(q_hbm, q_ref, load_sem.at[2]),
        pltpu.make_async_copy(start_hbm.at[place], start_ref, load_sem.at[3]),
        pltpu.make_async_copy(w_hbm, w_ref, load_sem.at[4]),
    ]
    for load in loads:
        load.start()

    recv3[:, FEAT:, :] = jnp.zeros((GROUP, LANES - FEAT, LANES), BF16)

    barrier = pltpu.get_barrier_semaphore()
    for step in range(1, GROUP):
        pl.semaphore_signal(
            barrier, inc=1, device_id=(base + lax.rem(place + step, GROUP), head), device_id_type=MESH
        )
    for step in range(1, GROUPS):
        pl.semaphore_signal(
            barrier, inc=1,
            device_id=(lax.rem(group + step, GROUPS) * GROUP + place, head), device_id_type=MESH,
        )
    up = lax.rem(head + 1, RING)
    down = lax.rem(head + RING - 1, RING)
    for peer in (up, down):
        pl.semaphore_signal(barrier, inc=1, device_id=(seq, peer), device_id_type=MESH)

    lane = lax.broadcasted_iota(jnp.int32, (TOK, LANES), 1)
    is_one = jnp.where(lane == HD, 1.0, 0.0).astype(F32)
    row_h = lax.broadcasted_iota(jnp.int32, (HALF, HALF), 0)
    col_h = lax.broadcasted_iota(jnp.int32, (HALF, HALF), 1)
    earlier_block = row_h // MINIBATCH_TOKENS > col_h // MINIBATCH_TOKENS
    same_chunk = row_h // HD == col_h // HD
    near_mask = jnp.logical_and(earlier_block, same_chunk)
    far_mask = jnp.logical_and(earlier_block, jnp.logical_not(same_chunk))
    causal = row_h >= col_h

    def with_one(pair, odd):
        wide = pair.astype(F32)
        if odd:
            wide = pltpu.roll(wide, HD, 1)
        return jnp.where(lane < HD, wide, is_one)

    def build_maps(slot, p):
        cols = pl.ds(pl.multiple_of(p * LANES, LANES), LANES)
        kp = k_ref[:, cols]
        vp = v_ref[:, cols]
        two = (0, 1)
        kf = [with_one(kp, e) for e in two]
        kx = [kf[e].astype(BF16) for e in two]
        ktf = [jnp.transpose(kf[e]) for e in two]
        kt = [ktf[e].astype(BF16) for e in two]
        rate = [rate_ref[pl.ds(2 * p + e, 1), :] for e in two]
        vx = [jnp.where((lane < HD) == (e == 0), vp.astype(F32), 0.0).astype(BF16) for e in two]
        x = [jnp.concatenate([kx[e], vx[e]], axis=1) for e in two]
        low = [dot(kx[e], kt[e]) * rate[e] for e in two]
        lows = [(low[e][:HALF, :HALF], low[e][HALF:, HALF:]) for e in two]
        cross = [low[e][HALF:, :HALF].astype(BF16) for e in two]
        both = [(e, b) for e in two for b in two]
        near = {eb: jnp.where(near_mask, lows[eb[0]][eb[1]], 0.0) for eb in both}
        far = {eb: jnp.where(far_mask, lows[eb[0]][eb[1]], 0.0) for eb in both}
        near_b = {eb: near[eb].astype(BF16) for eb in both}
        sq = {eb: dot(near_b[eb], near_b[eb]) for eb in both}
        n64 = {eb: sq[eb] - near[eb] - dot(near_b[eb], sq[eb].astype(BF16)) for eb in both}
        n64_b = {eb: n64[eb].astype(BF16) for eb in both}
        z = {eb: far[eb] + dot(n64_b[eb], far[eb].astype(BF16)) for eb in both}
        inv = {
            eb: (n64[eb] - z[eb] - dot(z[eb].astype(BF16), n64_b[eb])).astype(BF16) for eb in both
        }
        x0 = [x[e][:HALF] for e in two]
        u0 = [(x0[e].astype(F32) + dot(inv[e, 0], x0[e])).astype(BF16) for e in two]
        x1 = [x[e][HALF:].astype(F32) - dot(cross[e], u0[e]) for e in two]
        u1 = [(x1[e] + dot(inv[e, 1], x1[e].astype(BF16))).astype(BF16) for e in two]
        sign = jnp.where(
            lax.broadcasted_iota(jnp.int32, (FEAT, 2 * LANES), 1) < LANES, -1.0, 1.0
        ).astype(F32)
        for e in two:
            u = jnp.concatenate([u0[e], u1[e]], axis=0)
            u_ref[2 * p + e] = u
            kt_ref[2 * p + e] = kt[e]
            krt = (ktf[e][:FEAT] * rate[e]).astype(BF16)
            send1[slot, e] = (dot(krt, u) * sign).astype(BF16)

    def build_outputs(p):
        qp = q_ref[:, p * LANES : (p + 1) * LANES]
        total = None
        for e in (0, 1):
            qf = with_one(qp, e)
            scores = dot(qf.astype(BF16), kt_ref[2 * p + e]) * rate_ref[2 * p + e : 2 * p + e + 1, :]
            top = jnp.where(causal, scores[:HALF, :HALF], 0.0).astype(BF16)
            last = jnp.where(causal, scores[HALF:, HALF:], 0.0).astype(BF16)
            bottom = jnp.concatenate([scores[HALF:, :HALF].astype(BF16), last], axis=1)
            pu = jnp.concatenate(
                [dot(top, u_ref[2 * p + e, :HALF, :]), dot(bottom, u_ref[2 * p + e])], axis=0
            )
            qt_ref[p, :, e * LANES : (e + 1) * LANES] = (qf - pu[:, :LANES]).astype(BF16)
            total = pu[:, LANES:] if total is None else total + pu[:, LANES:]
        py_ref[p] = total

    def to_group(slot, e, peer):
        return pltpu.make_async_remote_copy(
            src_ref=send1.at[slot, e],
            dst_ref=recv1.at[place],
            send_sem=send_sem1.at[slot, e],
            recv_sem=recv_sem1.at[place],
            device_id=(base + peer, head),
            device_id_type=MESH,
        )

    copies = []
    loads[0].wait()
    loads[1].wait()
    for slot, step in enumerate((2, 1, 3, 0)):
        p = lax.rem(chip + step, PAIRS)
        build_maps(slot, p)
        if slot == 0:
            pl.semaphore_wait(barrier, GROUP - 1 + GROUPS - 1 + 2)
        if step:
            for e in (0, 1):
                copy = to_group(slot, e, 2 * p + e)
                copy.start()
                copies.append(copy)
        else:
            copy = to_group(slot, 1 - core, 2 * p + 1 - core)
            copy.start()
            copies.append(copy)
            recv1[place] = send1[slot, core]

    loads[2].wait()
    build_outputs(0)
    build_outputs(1)

    pad = jnp.zeros((LANES - FEAT, 2 * LANES), BF16)
    total = None
    for j in range(GROUP):
        @pl.when(place != j)
        def _(j=j):
            pltpu.make_async_remote_copy(
                src_ref=send1.at[0, 0],
                dst_ref=recv1.at[j],
                send_sem=send_sem1.at[0, 0],
                recv_sem=recv_sem1.at[j],
                device_id=(base + j, head),
                device_id_type=MESH,
            ).wait_recv()

        here = recv1[j]
        if total is None:
            total = here.astype(F32)
        else:
            rounded = total.astype(BF16)
            prefix[j - 1] = rounded
            total = total + here.astype(F32) + dot(
                here[:, :LANES], jnp.concatenate([rounded, pad], axis=0)
            )
    send2[...] = total.astype(BF16)

    def to_groups(step):
        return pltpu.make_async_remote_copy(
            src_ref=send2,
            dst_ref=recv2.at[group],
            send_sem=send_sem2.at[step - 1],
            recv_sem=recv_sem2.at[group],
            device_id=((group + step) * GROUP + place, head),
            device_id_type=MESH,
        )

    for step in range(1, GROUPS):
        @pl.when(group + step < GROUPS)
        def _(step=step):
            to_groups(step).start()

    build_outputs(2)

    loads[3].wait()
    first = jnp.concatenate([start_ref[...], jnp.zeros((HD, LANES - HD - 1), F32)], axis=1)
    nothing = jnp.zeros((HD, LANES), F32)
    stacked = jnp.concatenate(
        [jnp.where(core == 0, first, nothing), jnp.where(core == 1, first, nothing)], axis=0
    )
    state[...] = jnp.transpose(stacked)
    for g in range(GROUPS - 1):
        @pl.when(g < group)
        def _(g=g):
            pltpu.make_async_remote_copy(
                src_ref=send2,
                dst_ref=recv2.at[g],
                send_sem=send_sem2.at[0],
                recv_sem=recv_sem2.at[g],
                device_id=(g * GROUP + place, head),
                device_id_type=MESH,
            ).wait_recv()
            step_map = recv2[g]
            old = state[...]
            state[:FEAT, :] = (
                old[:FEAT]
                + step_map[:, LANES:].astype(F32)
                + dot(step_map[:, :LANES], old.astype(BF16))
            )

    entry = state[...]
    entry_b = entry.astype(BF16)
    send3[0] = entry_b[:FEAT]
    for j in range(1, GROUP):
        before = prefix[j - 1]
        send3[j] = (
            entry[:FEAT] + before[:, LANES:].astype(F32) + dot(before[:, :LANES], entry_b)
        ).astype(BF16)

    def back(step):
        peer = lax.rem(place + step, GROUP)
        return pltpu.make_async_remote_copy(
            src_ref=send3.at[peer],
            dst_ref=recv3.at[place, pl.ds(0, FEAT)],
            send_sem=send_sem3.at[step - 1],
            recv_sem=recv_sem3.at[place],
            device_id=(base + peer, head),
            device_id_type=MESH,
        )

    for step in (4, 5, 3, 2, 6, 7, 1):
        copy = back(step)
        copy.start()
        copies.append(copy)
    recv3[place, :FEAT, :] = send3[place]

    build_outputs(3)

    for step in range(1, GROUP):
        source = lax.rem(place + step, GROUP)
        pltpu.make_async_remote_copy(
            src_ref=send3.at[0],
            dst_ref=recv3.at[source, pl.ds(0, FEAT)],
            send_sem=send_sem3.at[0],
            recv_sem=recv_sem3.at[source],
            device_id=(base + source, head),
            device_id_type=MESH,
        ).wait_recv()
    loads[4].wait()

    states = [
        jnp.concatenate([recv3[2 * p], recv3[2 * p + 1]], axis=0) for p in range(PAIRS)
    ]

    def outputs_of(block):
        rows = pl.ds(pl.multiple_of(block * ROWS, ROWS), ROWS)
        return jnp.concatenate(
            [
                (dot(qt_ref[p, rows, :], states[p]) + py_ref[p, rows, :]).astype(BF16)
                for p in range(PAIRS)
            ],
            axis=1,
        )

    half = WIDTH // 2

    def project(z, side, piece):
        at = side * half + piece * 512
        return dot(z, w_ref[:, at : at + 512])

    def send(source, target, send_at, recv_at, peer):
        copy = pltpu.make_async_remote_copy(
            src_ref=source, dst_ref=target, send_sem=send_at, recv_sem=recv_at,
            device_id=(seq, peer), device_id_type=MESH,
        )
        copy.start()
        copies.append(copy)

    def arrived(target, recv_at, peer):
        pltpu.make_async_remote_copy(
            src_ref=far_send.at[0], dst_ref=target, send_sem=far_send_sem.at[0], recv_sem=recv_at,
            device_id=(seq, peer), device_id_type=MESH,
        ).wait_recv()

    z = outputs_of(lax.rem(head + 2, RING))
    for side, peer in ((0, up), (1, down)):
        for piece in (0, 1):
            far_send[side, :, piece * 512 : (piece + 1) * 512] = project(z, side, piece).astype(BF16)
        send(far_send.at[side], far_recv.at[side], far_send_sem.at[side], far_recv_sem.at[side], peer)
    z_near = [outputs_of(up), outputs_of(down)]
    for way, peer in ((0, up), (1, down)):
        side = 1 - way
        for piece in (0, 1):
            near_send[way, side, :, piece * 512 : (piece + 1) * 512] = project(
                z_near[way], side, piece
            ).astype(BF16)
        send(
            near_send.at[way, side], near_recv.at[way, side],
            near_send_sem.at[way, side], near_recv_sem.at[way, side], peer,
        )
    for way, peer, source in ((0, up, down), (1, down, up)):
        side = way
        arrived(far_recv.at[side], far_recv_sem.at[side], source)
        for piece in (0, 1):
            cols = slice(piece * 512, (piece + 1) * 512)
            near_send[way, side, :, cols] = (
                project(z_near[way], side, piece) + far_recv[side, :, cols].astype(F32)
            ).astype(BF16)
        send(
            near_send.at[way, side], near_recv.at[way, side],
            near_send_sem.at[way, side], near_recv_sem.at[way, side], peer,
        )
    z = outputs_of(head)
    own = [[project(z, side, piece) for piece in (0, 1)] for side in (0, 1)]
    for way, side in ((0, 1), (1, 0), (0, 0), (1, 1)):
        arrived(near_recv.at[way, side], near_recv_sem.at[way, side], down if way == 0 else up)
    for side in (0, 1):
        for piece in (0, 1):
            cols = slice(piece * 512, (piece + 1) * 512)
            at = side * half + piece * 512
            out_ref[:, at : at + 512] = (
                own[side][piece]
                + near_recv[0, side, :, cols].astype(F32)
                + near_recv[1, side, :, cols].astype(F32)
            ).astype(BF16)

    for copy in copies:
        copy.wait_send()
    for step in range(1, GROUPS):
        @pl.when(group + step < GROUPS)
        def _(step=step):
            to_groups(step).wait_send()


def per_device(queries, keys, values, rates, start_state, out_weight):
    hbm = pl.BlockSpec(memory_space=pl.ANY)
    vmem = pl.BlockSpec(memory_space=pltpu.VMEM)
    dma = pltpu.SemaphoreType.DMA
    half = WIDTH // 2
    return pl.pallas_call(
        kernel,
        out_shape=jax.ShapeDtypeStruct((ROWS, WIDTH), BF16),
        in_specs=[hbm, hbm, hbm, vmem, hbm, hbm],
        out_specs=vmem,
        scratch_shapes=[
            pltpu.VMEM((TOK, 8 * HD), BF16),
            pltpu.VMEM((TOK, 8 * HD), BF16),
            pltpu.VMEM((TOK, 8 * HD), BF16),
            pltpu.VMEM((8 * HD, WIDTH), BF16),
            pltpu.VMEM((HD, HD + 1), F32),
            pltpu.VMEM((2 * PAIRS, TOK, 2 * LANES), BF16),
            pltpu.VMEM((2 * PAIRS, LANES, TOK), BF16),
            pltpu.VMEM((PAIRS, TOK, 2 * LANES), BF16),
            pltpu.VMEM((PAIRS, TOK, LANES), F32),
            pltpu.VMEM((PAIRS, 2, FEAT, 2 * LANES), BF16),
            pltpu.VMEM((GROUP, FEAT, 2 * LANES), BF16),
            pltpu.VMEM((GROUP - 1, FEAT, 2 * LANES), BF16),
            pltpu.VMEM((FEAT, 2 * LANES), BF16),
            pltpu.VMEM((GROUPS, FEAT, 2 * LANES), BF16),
            pltpu.VMEM((LANES, LANES), F32),
            pltpu.VMEM((GROUP, FEAT, LANES), BF16),
            pltpu.VMEM((GROUP, LANES, LANES), BF16),
            pltpu.VMEM((2, ROWS, half), BF16),
            pltpu.VMEM((2, ROWS, half), BF16),
            pltpu.VMEM((2, 2, ROWS, half), BF16),
            pltpu.VMEM((2, 2, ROWS, half), BF16),
            dma((5,)),
            dma((PAIRS, 2)),
            dma((GROUP,)),
            dma((GROUPS - 1,)),
            dma((GROUPS,)),
            dma((GROUP - 1,)),
            dma((GROUP,)),
            dma((2,)),
            dma((2,)),
            dma((2, 2)),
            dma((2, 2)),
        ],
        compiler_params=pltpu.CompilerParams(
            collective_id=0, has_side_effects=True, vmem_limit_bytes=48 * 1024 * 1024
        ),
    )(queries, keys, values, jnp.transpose(rates), start_state, out_weight)


def solution(mesh):
    in_specs = (
        P("seq", "head"),
        P("seq", "head"),
        P("seq", "head"),
        P("seq", "head"),
        P("head", None, None),
        P("head", None),
    )
    out_specs = P(("seq", "head"), None)
    return jax.shard_map(
        per_device, mesh=mesh, in_specs=in_specs, out_specs=out_specs, check_vma=False
    )
```

```python
import jax
import jax.numpy as jnp
from jax import lax
from jax.experimental import pallas as pl
from jax.experimental.pallas import tpu as pltpu
from jax.sharding import PartitionSpec as P

HD = 64
MINIBATCH_TOKENS = 16
TOK = 256
HALF = TOK // 2
PAIRS = 4
GROUP = 8
GROUPS = 4
RING = 4
FEAT = 80
LANES = 128
PACKED = 48
WIDTH = 2048
ROWS = TOK // RING
CHUNKS = 4
CHUNK = ROWS // CHUNKS
MESH = pl.DeviceIdType.MESH
F32 = jnp.float32
BF16 = jnp.bfloat16


def dot(left, right):
    return jnp.dot(left, right, preferred_element_type=F32)


def dot_t(left, right):
    return lax.dot_general(left, right, (((1,), (1,)), ((), ())), preferred_element_type=F32)


def kernel(
    q_hbm, k_hbm, v_hbm, rate_hbm, start_hbm, w_hbm, out_ref,
    q_ref, k_ref, v_ref, w_ref, start_ref, rate_ref,
    u_ref, kt_ref, qt_ref, py_ref,
    send1, recv1, prefix, send2, recv2, send3, recv3,
    far_send, far_recv, near_send, near_recv,
    load_sem, send_sem1, recv_sem1, send_sem2, recv_sem2, send_sem3, recv_sem3,
    far_send_sem, far_recv_sem, near_send_sem, near_recv_sem, merge_send_sem, merge_recv_sem,
):
    seq = lax.axis_index("seq")
    head = lax.axis_index("head")
    group = seq // GROUP
    place = lax.rem(seq, GROUP)
    chip = place // 2
    core = lax.rem(place, 2)
    base = group * GROUP

    loads = [
        pltpu.make_async_copy(k_hbm, k_ref, load_sem.at[0]),
        pltpu.make_async_copy(v_hbm, v_ref, load_sem.at[1]),
        pltpu.make_async_copy(q_hbm, q_ref, load_sem.at[2]),
        pltpu.make_async_copy(start_hbm.at[place], start_ref, load_sem.at[3]),
        pltpu.make_async_copy(w_hbm, w_ref, load_sem.at[4]),
        pltpu.make_async_copy(rate_hbm, rate_ref, load_sem.at[5]),
    ]
    for load in (loads[5], loads[0], loads[1]):
        load.start()

    barrier = pltpu.get_barrier_semaphore()
    for step in range(1, GROUP):
        pl.semaphore_signal(
            barrier, inc=1, device_id=(base + lax.rem(place + step, GROUP), head), device_id_type=MESH
        )
    for step in range(1, GROUPS):
        pl.semaphore_signal(
            barrier, inc=1,
            device_id=(lax.rem(group + step, GROUPS) * GROUP + place, head), device_id_type=MESH,
        )
    up = lax.rem(head + 1, RING)
    down = lax.rem(head + RING - 1, RING)
    for peer in (up, down):
        pl.semaphore_signal(barrier, inc=1, device_id=(seq, peer), device_id_type=MESH)

    lane = lax.broadcasted_iota(jnp.int32, (TOK, LANES), 1)
    is_one = jnp.where(lane == HD, 1.0, 0.0).astype(F32)
    row_h = lax.broadcasted_iota(jnp.int32, (HALF, HALF), 0)
    col_h = lax.broadcasted_iota(jnp.int32, (HALF, HALF), 1)
    earlier_block = row_h // MINIBATCH_TOKENS > col_h // MINIBATCH_TOKENS
    same_chunk = row_h // HD == col_h // HD
    near_mask = jnp.logical_and(earlier_block, same_chunk)
    far_mask = jnp.logical_and(earlier_block, jnp.logical_not(same_chunk))
    causal = row_h >= col_h

    one_b = is_one.astype(BF16)
    lane_f = lane[:FEAT]
    row_f = lax.broadcasted_iota(jnp.int32, (FEAT, LANES), 0)
    sign = jnp.where(lane_f < HD, -1.0, 1.0).astype(F32)
    lane_t = lane[:16]
    row_t = lax.broadcasted_iota(jnp.int32, (16, LANES), 0)
    pick = jnp.where(jnp.logical_and(row_t == 1, lane_t == HD), 1.0, 0.0).astype(BF16)
    diagonal = jnp.where(row_f == lane_f, 1.0, 0.0).astype(BF16)
    rest = jnp.zeros((LANES - FEAT, LANES), BF16)

    def pack(wide, column):
        in_row = dot_t(pick, jnp.concatenate([column.astype(BF16), rest], axis=0))
        return jnp.concatenate([wide[:HD], wide[HD:] + in_row], axis=0).astype(BF16)

    def unpack(packed):
        wide = packed.astype(F32)
        in_row = jnp.where(row_t == 0, pltpu.roll(wide[HD:], 15, 0), 0.0).astype(BF16)
        column = dot_t(
            diagonal, jnp.concatenate([jnp.zeros((HD, LANES), BF16), in_row, rest], axis=0)
        )
        wide = jnp.where(row_f <= HD, wide, 0.0)
        return (
            jnp.where(lane_f < HD, wide, column).astype(BF16),
            jnp.concatenate([wide, column], axis=1),
        )

    def with_one(pair, odd):
        wide = pair.astype(F32)
        if odd:
            wide = pltpu.roll(wide, HD, 1)
        return jnp.where(lane < HD, wide, is_one)

    def build_maps(slots, pairs):
        heads = [(i, e) for i in range(len(pairs)) for e in (0, 1)]
        at = {h: 2 * pairs[h[0]] + h[1] for h in heads}
        cols = [pl.ds(pl.multiple_of(p * LANES, LANES), LANES) for p in pairs]
        kp = [k_ref[:, c] for c in cols]
        vp = [v_ref[:, c].astype(F32) for c in cols]
        vf = {h: vp[h[0]] if h[1] else pltpu.roll(vp[h[0]], HD, 1) for h in heads}
        kf = {h: with_one(kp[h[0]], h[1]) for h in heads}
        kx = {h: kf[h].astype(BF16) for h in heads}
        ktf = {h: jnp.transpose(kf[h]) for h in heads}
        kt = {h: ktf[h].astype(BF16) for h in heads}
        rate = {h: rate_ref[pl.ds(at[h], 1), :] for h in heads}
        x = {
            h: jnp.concatenate([jnp.where(lane < HD, kf[h], vf[h]).astype(BF16), one_b], axis=1)
            for h in heads
        }
        low = {h: dot(kx[h], kt[h]) * rate[h] for h in heads}
        lows = {h: (low[h][:HALF, :HALF], low[h][HALF:, HALF:]) for h in heads}
        cross = {h: low[h][HALF:, :HALF].astype(BF16) for h in heads}
        both = [(h, b) for h in heads for b in (0, 1)]
        near = {hb: jnp.where(near_mask, lows[hb[0]][hb[1]], 0.0) for hb in both}
        far = {hb: jnp.where(far_mask, lows[hb[0]][hb[1]], 0.0) for hb in both}
        near_b = {hb: near[hb].astype(BF16) for hb in both}
        sq = {hb: dot(near_b[hb], near_b[hb]) for hb in both}
        n64 = {hb: sq[hb] - near[hb] - dot(near_b[hb], sq[hb].astype(BF16)) for hb in both}
        n64_b = {hb: n64[hb].astype(BF16) for hb in both}
        z = {hb: far[hb] + dot(n64_b[hb], far[hb].astype(BF16)) for hb in both}
        inv = {
            hb: (n64[hb] - z[hb] - dot(z[hb].astype(BF16), n64_b[hb])).astype(BF16) for hb in both
        }
        x0 = {h: x[h][:HALF] for h in heads}
        u0 = {h: (x0[h].astype(F32) + dot(inv[h, 0], x0[h])).astype(BF16) for h in heads}
        x1 = {h: x[h][HALF:].astype(F32) - dot(cross[h], u0[h]) for h in heads}
        u1 = {h: (x1[h] + dot(inv[h, 1], x1[h].astype(BF16))).astype(BF16) for h in heads}
        u = {h: jnp.concatenate([u0[h], u1[h]], axis=0) for h in heads}
        krt = {h: (ktf[h][:FEAT] * rate[h]).astype(BF16) for h in heads}
        maps = {h: dot(krt[h], u[h]) for h in heads}
        for h in heads:
            send1[slots[h[0]], h[1]] = pack(maps[h][:, :LANES] * sign, -maps[h][:, LANES:])
        for h in heads:
            u_ref[at[h]] = u[h]
            kt_ref[at[h]] = kt[h]

    def build_outputs(p):
        qp = q_ref[:, p * LANES : (p + 1) * LANES]
        for e in (0, 1):
            qf = with_one(qp, e)
            scores = dot(qf.astype(BF16), kt_ref[2 * p + e]) * rate_ref[2 * p + e : 2 * p + e + 1, :]
            top = jnp.where(causal, scores[:HALF, :HALF], 0.0).astype(BF16)
            last = jnp.where(causal, scores[HALF:, HALF:], 0.0).astype(BF16)
            bottom = jnp.concatenate([scores[HALF:, :HALF].astype(BF16), last], axis=1)
            pu = jnp.concatenate(
                [dot(top, u_ref[2 * p + e, :HALF, :]), dot(bottom, u_ref[2 * p + e])], axis=0
            )
            qt_ref[p, :, e * LANES : (e + 1) * LANES] = jnp.where(
                lane < HD, qf - pu[:, :LANES], is_one - pu[:, LANES:]
            ).astype(BF16)
            if e == 0:
                total = pltpu.roll(pu[:, :LANES], HD, 1)
            else:
                py_ref[p] = jnp.where(lane < HD, total, pu[:, :LANES])

    def to_group(slot, e, peer):
        return pltpu.make_async_remote_copy(
            src_ref=send1.at[slot, e],
            dst_ref=recv1.at[place],
            send_sem=send_sem1.at[slot, e],
            recv_sem=recv_sem1.at[place],
            device_id=(base + peer, head),
            device_id_type=MESH,
        )

    copies = []
    for load in (loads[5], loads[0], loads[1]):
        load.wait()
    for load in loads[2:5]:
        load.start()
    steps = (2, 1, 3, 0)
    for batch in ((0, 1), (2, 3)):
        pairs = [lax.rem(chip + steps[slot], PAIRS) for slot in batch]
        build_maps(batch, pairs)
        if batch[0] == 0:
            pl.semaphore_wait(barrier, GROUP - 1 + GROUPS - 1 + 2)
        for slot, p in zip(batch, pairs):
            if steps[slot]:
                for e in (0, 1):
                    copy = to_group(slot, e, 2 * p + e)
                    copy.start()
                    copies.append(copy)
            else:
                copy = to_group(slot, 1 - core, 2 * p + 1 - core)
                copy.start()
                copies.append(copy)
                recv1[place] = send1[slot, core]

    loads[2].wait()
    build_outputs(0)
    build_outputs(1)

    pad = jnp.zeros((LANES - FEAT, 2 * LANES), BF16)
    for j in range(GROUP):
        @pl.when(place != j)
        def _(j=j):
            pltpu.make_async_remote_copy(
                src_ref=send1.at[0, 0],
                dst_ref=recv1.at[j],
                send_sem=send_sem1.at[0, 0],
                recv_sem=recv_sem1.at[j],
                device_id=(base + j, head),
                device_id_type=MESH,
            ).wait_recv()

    def as_left(step_map):
        return jnp.where(lane_f < HD, step_map[:, :LANES], step_map[:, LANES:]).astype(BF16)

    def then(earlier, left, later):
        padded = jnp.concatenate([earlier.astype(BF16), pad], axis=0)
        return earlier + later + dot(left, padded)

    lefts, maps = zip(*[unpack(recv1[j]) for j in range(GROUP)])
    m01, m23, m45, m67 = [then(maps[j], lefts[j + 1], maps[j + 1]) for j in (0, 2, 4, 6)]
    m03 = then(m01, as_left(m23), m23)
    m47 = then(m45, as_left(m67), m67)
    m07 = then(m03, as_left(m47), m47)
    send2[...] = pack(m07[:, :LANES], m07[:, LANES:])

    def to_groups(step):
        return pltpu.make_async_remote_copy(
            src_ref=send2,
            dst_ref=recv2.at[group],
            send_sem=send_sem2.at[step - 1],
            recv_sem=recv_sem2.at[group],
            device_id=((group + step) * GROUP + place, head),
            device_id_type=MESH,
        )

    for step in range(1, GROUPS):
        @pl.when(group + step < GROUPS)
        def _(step=step):
            to_groups(step).start()

    m02 = then(m01, lefts[2], maps[2])
    m04 = then(m03, lefts[4], maps[4])
    m05 = then(m03, as_left(m45), m45)
    m46 = then(m45, lefts[6], maps[6])
    m06 = then(m03, as_left(m46), m46)
    for j, step_map in enumerate((maps[0], m01, m02, m03, m04, m05, m06)):
        prefix[j] = step_map.astype(BF16)
    build_outputs(2)

    loads[3].wait()
    first = jnp.concatenate([start_ref[...], jnp.zeros((HD, LANES - HD - 1), F32)], axis=1)
    entry = jnp.transpose(jnp.concatenate([jnp.zeros((HD, LANES), F32), first], axis=0))[:FEAT]
    for g in range(GROUPS - 1):
        @pl.when(g < group)
        def _(g=g):
            pltpu.make_async_remote_copy(
                src_ref=send2,
                dst_ref=recv2.at[g],
                send_sem=send_sem2.at[0],
                recv_sem=recv_sem2.at[g],
                device_id=(g * GROUP + place, head),
                device_id_type=MESH,
            ).wait_recv()

    half_pad = jnp.zeros((LANES - FEAT, LANES), BF16)

    def apply(left, step_map, old):
        padded = jnp.concatenate([old.astype(BF16), half_pad], axis=0)
        return old + jnp.where(lane_f < HD, 0.0, step_map) + dot(left, padded)

    passed = [
        unpack(jnp.where(g < group, recv2[g].astype(F32), 0.0)) for g in range(GROUPS - 1)
    ]
    for left, step_map in passed:
        entry = apply(left, step_map[:, :LANES], entry)

    def pack_state(rows):
        return jnp.concatenate(
            [
                jnp.where(lane[:32] < HD, pltpu.roll(rows[:32], HD, 1), rows[32:HD]),
                rows[HD:],
            ],
            axis=0,
        ).astype(BF16)

    send3[0] = pack_state(entry)
    for j in range(1, GROUP):
        before = prefix[j - 1].astype(F32)
        send3[j] = pack_state(apply(as_left(before), before[:, :LANES], entry))

    def back(step):
        peer = lax.rem(place + step, GROUP)
        return pltpu.make_async_remote_copy(
            src_ref=send3.at[peer],
            dst_ref=recv3.at[place],
            send_sem=send_sem3.at[step - 1],
            recv_sem=recv_sem3.at[place],
            device_id=(base + peer, head),
            device_id_type=MESH,
        )

    for step in (4, 5, 3, 2, 6, 7, 1):
        copy = back(step)
        copy.start()
        copies.append(copy)
    recv3[place] = send3[place]

    build_outputs(3)

    for step in range(1, GROUP):
        source = lax.rem(place + step, GROUP)
        pltpu.make_async_remote_copy(
            src_ref=send3.at[0],
            dst_ref=recv3.at[source],
            send_sem=send_sem3.at[0],
            recv_sem=recv_sem3.at[source],
            device_id=(base + source, head),
            device_id_type=MESH,
        ).wait_recv()
    loads[4].wait()

    def unpack_state(h):
        wide = recv3[h].astype(F32)
        turned = pltpu.roll(wide, HD, 1)
        odd = h % 2
        ours = (lane[: PACKED] < HD) != (odd == 1)
        same = jnp.where(ours, wide, 0.0)
        other = jnp.where(ours, turned, 0.0)
        if odd:
            parts = [other[:32], same[:32], same[32:]]
        else:
            parts = [same[:32], other[:32], other[32:]]
        return jnp.concatenate([jnp.concatenate(parts, axis=0).astype(BF16), rest], axis=0)

    states = [
        jnp.concatenate([unpack_state(2 * p), unpack_state(2 * p + 1)], axis=0)
        for p in range(PAIRS)
    ]

    def outputs_of(block):
        rows = pl.ds(pl.multiple_of(block * ROWS, ROWS), ROWS)
        return jnp.concatenate(
            [
                (dot(qt_ref[p, rows, :], states[p]) + py_ref[p, rows, :]).astype(BF16)
                for p in range(PAIRS)
            ],
            axis=1,
        )

    half = WIDTH // 2

    def project(z, side, piece):
        at = side * half + piece * 512
        return dot(z, w_ref[:, at : at + 512])

    def send(source, target, send_at, recv_at, peer):
        copy = pltpu.make_async_remote_copy(
            src_ref=source, dst_ref=target, send_sem=send_at, recv_sem=recv_at,
            device_id=(seq, peer), device_id_type=MESH,
        )
        copy.start()
        return copy

    def arrived(target, recv_at, peer):
        pltpu.make_async_remote_copy(
            src_ref=target, dst_ref=target, send_sem=far_send_sem.at[0, 0], recv_sem=recv_at,
            device_id=(seq, peer), device_id_type=MESH,
        ).wait_recv()

    chunks = range(CHUNKS)

    def chunk_rows(chunk):
        return pl.ds(chunk * CHUNK, CHUNK)

    z = outputs_of(lax.rem(head + 2, RING))
    for side, peer in ((0, up), (1, down)):
        for piece in (0, 1):
            far_send[side, :, piece * 512 : (piece + 1) * 512] = project(z, side, piece).astype(BF16)
        for chunk in chunks:
            copies.append(
                send(
                    far_send.at[side, chunk_rows(chunk)], far_recv.at[side, chunk_rows(chunk)],
                    far_send_sem.at[side, chunk], far_recv_sem.at[side, chunk], peer,
                )
            )
    z_near = [outputs_of(up), outputs_of(down)]
    def send_near(way, side, peer):
        copies.append(
            send(
                near_send.at[way, side], near_recv.at[way, side],
                near_send_sem.at[way], near_recv_sem.at[way], peer,
            )
        )

    for way in (0, 1):
        side = 1 - way
        for piece in (0, 1):
            near_send[way, side, :, piece * 512 : (piece + 1) * 512] = project(
                z_near[way], side, piece
            ).astype(BF16)
        send_near(way, side, (up, down)[way])
    merged = [[project(z_near[way], way, piece) for piece in (0, 1)] for way in (0, 1)]
    for chunk in chunks:
        for way, peer, source in ((0, up, down), (1, down, up)):
            rows = chunk_rows(chunk)
            arrived(far_recv.at[way, rows], far_recv_sem.at[way, chunk], source)
            for piece in (0, 1):
                cols = slice(piece * 512, (piece + 1) * 512)
                near_send[way, way, rows, cols] = (
                    merged[way][piece][chunk * CHUNK : (chunk + 1) * CHUNK]
                    + far_recv[way, rows, cols].astype(F32)
                ).astype(BF16)
            copies.append(
                send(
                    near_send.at[way, way, rows], near_recv.at[way, way, rows],
                    merge_send_sem.at[way, chunk], merge_recv_sem.at[way, chunk], peer,
                )
            )
    z = outputs_of(head)
    own = [[project(z, side, piece) for piece in (0, 1)] for side in (0, 1)]
    sources = (down, up)
    for way in (0, 1):
        arrived(near_recv.at[way, 1 - way], near_recv_sem.at[way], sources[way])
    for chunk in chunks:
        for way in (0, 1):
            arrived(
                near_recv.at[way, way, chunk_rows(chunk)], merge_recv_sem.at[way, chunk], sources[way]
            )
    for side in (0, 1):
        for piece in (0, 1):
            cols = slice(piece * 512, (piece + 1) * 512)
            at = side * half + piece * 512
            out_ref[:, at : at + 512] = (
                own[side][piece]
                + near_recv[0, side, :, cols].astype(F32)
                + near_recv[1, side, :, cols].astype(F32)
            ).astype(BF16)

    for copy in copies:
        copy.wait_send()
    for step in range(1, GROUPS):
        @pl.when(group + step < GROUPS)
        def _(step=step):
            to_groups(step).wait_send()


def per_device(queries, keys, values, rates, start_state, out_weight):
    hbm = pl.BlockSpec(memory_space=pl.ANY)
    vmem = pl.BlockSpec(memory_space=pltpu.VMEM)
    dma = pltpu.SemaphoreType.DMA
    half = WIDTH // 2
    return pl.pallas_call(
        kernel,
        out_shape=jax.ShapeDtypeStruct((ROWS, WIDTH), BF16),
        in_specs=[hbm] * 6,
        out_specs=vmem,
        scratch_shapes=[
            pltpu.VMEM((TOK, 8 * HD), BF16),
            pltpu.VMEM((TOK, 8 * HD), BF16),
            pltpu.VMEM((TOK, 8 * HD), BF16),
            pltpu.VMEM((8 * HD, WIDTH), BF16),
            pltpu.VMEM((HD, HD + 1), F32),
            pltpu.VMEM((2 * PAIRS, TOK), F32),
            pltpu.VMEM((2 * PAIRS, TOK, 2 * LANES), BF16),
            pltpu.VMEM((2 * PAIRS, LANES, TOK), BF16),
            pltpu.VMEM((PAIRS, TOK, 2 * LANES), BF16),
            pltpu.VMEM((PAIRS, TOK, LANES), F32),
            pltpu.VMEM((PAIRS, 2, FEAT, LANES), BF16),
            pltpu.VMEM((GROUP, FEAT, LANES), BF16),
            pltpu.VMEM((GROUP - 1, FEAT, 2 * LANES), BF16),
            pltpu.VMEM((FEAT, LANES), BF16),
            pltpu.VMEM((GROUPS, FEAT, LANES), BF16),
            pltpu.VMEM((GROUP, PACKED, LANES), BF16),
            pltpu.VMEM((GROUP, PACKED, LANES), BF16),
            pltpu.VMEM((2, ROWS, half), BF16),
            pltpu.VMEM((2, ROWS, half), BF16),
            pltpu.VMEM((2, 2, ROWS, half), BF16),
            pltpu.VMEM((2, 2, ROWS, half), BF16),
            dma((6,)),
            dma((PAIRS, 2)),
            dma((GROUP,)),
            dma((GROUPS - 1,)),
            dma((GROUPS,)),
            dma((GROUP - 1,)),
            dma((GROUP,)),
            dma((2, CHUNKS)),
            dma((2, CHUNKS)),
            dma((2,)),
            dma((2,)),
            dma((2, CHUNKS)),
            dma((2, CHUNKS)),
        ],
        compiler_params=pltpu.CompilerParams(
            collective_id=0, has_side_effects=True, vmem_limit_bytes=60 * 1024 * 1024
        ),
    )(queries, keys, values, jnp.transpose(rates), start_state, out_weight)


def solution(mesh):
    in_specs = (
        P("seq", "head"),
        P("seq", "head"),
        P("seq", "head"),
        P("seq", "head"),
        P("head", None, None),
        P("head", None),
    )
    out_specs = P(("seq", "head"), None)
    return jax.shard_map(
        per_device, mesh=mesh, in_specs=in_specs, out_specs=out_specs, check_vma=False
    )
```

```python
import jax
import jax.numpy as jnp
from jax import lax
from jax.experimental import pallas as pl
from jax.experimental.pallas import tpu as pltpu
from jax.sharding import PartitionSpec as P

HD = 64
MINIBATCH_TOKENS = 16
TOK = 256
HALF = TOK // 2
PAIRS = 4
GROUP = 8
GROUPS = 4
RING = 4
FEAT = 80
LANES = 128
PACKED = 48
WIDTH = 2048
ROWS = TOK // RING
CHUNKS = 4
CHUNK = ROWS // CHUNKS
MESH = pl.DeviceIdType.MESH
F32 = jnp.float32
BF16 = jnp.bfloat16


def dot(left, right):
    return jnp.dot(left, right, preferred_element_type=F32)


def dot_t(left, right):
    return lax.dot_general(left, right, (((1,), (1,)), ((), ())), preferred_element_type=F32)


def kernel(
    q_hbm, k_hbm, v_hbm, rate_hbm, start_hbm, w_hbm, out_ref,
    q_ref, k_ref, v_ref, w_ref, start_ref, rate_ref,
    u_ref, kt_ref, qt_ref, py_ref,
    send1, recv1, prefix, send2, recv2, send3, recv3,
    far_send, far_recv, near_send, near_recv,
    load_sem, send_sem1, recv_sem1, send_sem2, recv_sem2, send_sem3, recv_sem3,
    far_send_sem, far_recv_sem, near_send_sem, near_recv_sem, merge_send_sem, merge_recv_sem,
):
    seq = lax.axis_index("seq")
    head = lax.axis_index("head")
    group = seq // GROUP
    place = lax.rem(seq, GROUP)
    chip = place // 2
    core = lax.rem(place, 2)
    base = group * GROUP

    loads = [
        pltpu.make_async_copy(k_hbm, k_ref, load_sem.at[0]),
        pltpu.make_async_copy(v_hbm, v_ref, load_sem.at[1]),
        pltpu.make_async_copy(q_hbm, q_ref, load_sem.at[2]),
        pltpu.make_async_copy(start_hbm.at[place], start_ref, load_sem.at[3]),
        pltpu.make_async_copy(w_hbm, w_ref, load_sem.at[4]),
        pltpu.make_async_copy(rate_hbm, rate_ref, load_sem.at[5]),
    ]
    for load in (loads[5], loads[0], loads[1]):
        load.start()

    barrier = pltpu.get_barrier_semaphore()
    for step in range(1, GROUP):
        pl.semaphore_signal(
            barrier, inc=1, device_id=(base + lax.rem(place + step, GROUP), head), device_id_type=MESH
        )
    for step in range(1, GROUPS):
        pl.semaphore_signal(
            barrier, inc=1,
            device_id=(lax.rem(group + step, GROUPS) * GROUP + place, head), device_id_type=MESH,
        )
    up = lax.rem(head + 1, RING)
    down = lax.rem(head + RING - 1, RING)
    for peer in (up, down):
        pl.semaphore_signal(barrier, inc=1, device_id=(seq, peer), device_id_type=MESH)

    lane = lax.broadcasted_iota(jnp.int32, (TOK, LANES), 1)
    is_one = jnp.where(lane == HD, 1.0, 0.0).astype(F32)
    row_h = lax.broadcasted_iota(jnp.int32, (HALF, HALF), 0)
    col_h = lax.broadcasted_iota(jnp.int32, (HALF, HALF), 1)
    earlier_block = row_h // MINIBATCH_TOKENS > col_h // MINIBATCH_TOKENS
    same_chunk = row_h // HD == col_h // HD
    near_mask = jnp.logical_and(earlier_block, same_chunk)
    far_mask = jnp.logical_and(earlier_block, jnp.logical_not(same_chunk))
    causal = row_h >= col_h

    one_b = is_one.astype(BF16)
    lane_f = lane[:FEAT]
    row_f = lax.broadcasted_iota(jnp.int32, (FEAT, LANES), 0)
    sign = jnp.where(lane_f < HD, -1.0, 1.0).astype(F32)
    lane_t = lane[:16]
    row_t = lax.broadcasted_iota(jnp.int32, (16, LANES), 0)
    pick = jnp.where(jnp.logical_and(row_t == 1, lane_t == HD), 1.0, 0.0).astype(BF16)
    diagonal = jnp.where(row_f == lane_f, 1.0, 0.0).astype(BF16)
    rest = jnp.zeros((LANES - FEAT, LANES), BF16)

    def pack(wide, column):
        in_row = dot_t(pick, jnp.concatenate([column.astype(BF16), rest], axis=0))
        return jnp.concatenate([wide[:HD], wide[HD:] + in_row], axis=0).astype(BF16)

    def unpack(packed):
        wide = packed.astype(F32)
        in_row = jnp.where(row_t == 0, pltpu.roll(wide[HD:], 15, 0), 0.0).astype(BF16)
        column = dot_t(
            diagonal, jnp.concatenate([jnp.zeros((HD, LANES), BF16), in_row, rest], axis=0)
        )
        wide = jnp.where(row_f <= HD, wide, 0.0)
        return (
            jnp.where(lane_f < HD, wide, column).astype(BF16),
            jnp.concatenate([wide, column], axis=1),
        )

    def with_one(pair, odd):
        wide = pair.astype(F32)
        if odd:
            wide = pltpu.roll(wide, HD, 1)
        return jnp.where(lane < HD, wide, is_one)

    def build_maps(slots, pairs):
        heads = [(i, e) for i in range(len(pairs)) for e in (0, 1)]
        at = {h: 2 * pairs[h[0]] + h[1] for h in heads}
        cols = [pl.ds(pl.multiple_of(p * LANES, LANES), LANES) for p in pairs]
        kp = [k_ref[:, c] for c in cols]
        vp = [v_ref[:, c].astype(F32) for c in cols]
        vf = {h: vp[h[0]] if h[1] else pltpu.roll(vp[h[0]], HD, 1) for h in heads}
        kf = {h: with_one(kp[h[0]], h[1]) for h in heads}
        kx = {h: kf[h].astype(BF16) for h in heads}
        ktf = {h: jnp.transpose(kf[h]) for h in heads}
        kt = {h: ktf[h].astype(BF16) for h in heads}
        rate = {h: rate_ref[pl.ds(at[h], 1), :] for h in heads}
        x = {
            h: jnp.concatenate([jnp.where(lane < HD, kf[h], vf[h]).astype(BF16), one_b], axis=1)
            for h in heads
        }
        low = {h: dot(kx[h], kt[h]) * rate[h] for h in heads}
        lows = {h: (low[h][:HALF, :HALF], low[h][HALF:, HALF:]) for h in heads}
        cross = {h: low[h][HALF:, :HALF].astype(BF16) for h in heads}
        both = [(h, b) for h in heads for b in (0, 1)]
        near = {hb: jnp.where(near_mask, lows[hb[0]][hb[1]], 0.0) for hb in both}
        far = {hb: jnp.where(far_mask, lows[hb[0]][hb[1]], 0.0) for hb in both}
        near_b = {hb: near[hb].astype(BF16) for hb in both}
        sq = {hb: dot(near_b[hb], near_b[hb]) for hb in both}
        n64 = {hb: sq[hb] - near[hb] - dot(near_b[hb], sq[hb].astype(BF16)) for hb in both}
        n64_b = {hb: n64[hb].astype(BF16) for hb in both}
        z = {hb: far[hb] + dot(n64_b[hb], far[hb].astype(BF16)) for hb in both}
        inv = {
            hb: (n64[hb] - z[hb] - dot(z[hb].astype(BF16), n64_b[hb])).astype(BF16) for hb in both
        }
        x0 = {h: x[h][:HALF] for h in heads}
        u0 = {h: (x0[h].astype(F32) + dot(inv[h, 0], x0[h])).astype(BF16) for h in heads}
        x1 = {h: x[h][HALF:].astype(F32) - dot(cross[h], u0[h]) for h in heads}
        u1 = {h: (x1[h] + dot(inv[h, 1], x1[h].astype(BF16))).astype(BF16) for h in heads}
        u = {h: jnp.concatenate([u0[h], u1[h]], axis=0) for h in heads}
        krt = {h: (ktf[h][:FEAT] * rate[h]).astype(BF16) for h in heads}
        maps = {h: dot(krt[h], u[h]) for h in heads}
        for h in heads:
            send1[slots[h[0]], h[1]] = pack(maps[h][:, :LANES] * sign, -maps[h][:, LANES:])
        for h in heads:
            u_ref[at[h]] = u[h]
            kt_ref[at[h]] = kt[h]

    def build_outputs(p):
        qp = q_ref[:, p * LANES : (p + 1) * LANES]
        for e in (0, 1):
            qf = with_one(qp, e)
            scores = dot(qf.astype(BF16), kt_ref[2 * p + e]) * rate_ref[2 * p + e : 2 * p + e + 1, :]
            top = jnp.where(causal, scores[:HALF, :HALF], 0.0).astype(BF16)
            last = jnp.where(causal, scores[HALF:, HALF:], 0.0).astype(BF16)
            bottom = jnp.concatenate([scores[HALF:, :HALF].astype(BF16), last], axis=1)
            pu = jnp.concatenate(
                [dot(top, u_ref[2 * p + e, :HALF, :]), dot(bottom, u_ref[2 * p + e])], axis=0
            )
            qt_ref[p, :, e * LANES : (e + 1) * LANES] = jnp.where(
                lane < HD, qf - pu[:, :LANES], is_one - pu[:, LANES:]
            ).astype(BF16)
            if e == 0:
                total = pltpu.roll(pu[:, :LANES], HD, 1)
            else:
                py_ref[p] = jnp.where(lane < HD, total, pu[:, :LANES])

    def to_group(slot, e, peer):
        return pltpu.make_async_remote_copy(
            src_ref=send1.at[slot, e],
            dst_ref=recv1.at[place],
            send_sem=send_sem1.at[slot, e],
            recv_sem=recv_sem1.at[place],
            device_id=(base + peer, head),
            device_id_type=MESH,
        )

    copies = []
    for load in (loads[5], loads[0], loads[1]):
        load.wait()
    for load in loads[2:5]:
        load.start()
    steps = (2, 1, 3, 0)
    for batch in ((0, 1), (2, 3)):
        pairs = [lax.rem(chip + steps[slot], PAIRS) for slot in batch]
        build_maps(batch, pairs)
        if batch[0] == 0:
            pl.semaphore_wait(barrier, GROUP - 1 + GROUPS - 1 + 2)
        for slot, p in zip(batch, pairs):
            if steps[slot]:
                for e in (0, 1):
                    copy = to_group(slot, e, 2 * p + e)
                    copy.start()
                    copies.append(copy)
            else:
                copy = to_group(slot, 1 - core, 2 * p + 1 - core)
                copy.start()
                copies.append(copy)
                recv1[place] = send1[slot, core]

    loads[2].wait()
    build_outputs(0)
    build_outputs(1)

    pad = jnp.zeros((LANES - FEAT, 2 * LANES), BF16)
    for j in range(GROUP):
        @pl.when(place != j)
        def _(j=j):
            pltpu.make_async_remote_copy(
                src_ref=send1.at[0, 0],
                dst_ref=recv1.at[j],
                send_sem=send_sem1.at[0, 0],
                recv_sem=recv_sem1.at[j],
                device_id=(base + j, head),
                device_id_type=MESH,
            ).wait_recv()

    def as_left(step_map):
        return jnp.where(lane_f < HD, step_map[:, :LANES], step_map[:, LANES:]).astype(BF16)

    def then(earlier, left, later):
        padded = jnp.concatenate([earlier.astype(BF16), pad], axis=0)
        return earlier + later + dot(left, padded)

    lefts, maps = zip(*[unpack(recv1[j]) for j in range(GROUP)])
    m01, m23, m45, m67 = [then(maps[j], lefts[j + 1], maps[j + 1]) for j in (0, 2, 4, 6)]
    m03 = then(m01, as_left(m23), m23)
    m47 = then(m45, as_left(m67), m67)
    m07 = then(m03, as_left(m47), m47)
    send2[...] = pack(m07[:, :LANES], m07[:, LANES:])

    def to_groups(step):
        return pltpu.make_async_remote_copy(
            src_ref=send2,
            dst_ref=recv2.at[group],
            send_sem=send_sem2.at[step - 1],
            recv_sem=recv_sem2.at[group],
            device_id=((group + step) * GROUP + place, head),
            device_id_type=MESH,
        )

    for step in range(1, GROUPS):
        @pl.when(group + step < GROUPS)
        def _(step=step):
            to_groups(step).start()

    m02 = then(m01, lefts[2], maps[2])
    m04 = then(m03, lefts[4], maps[4])
    m05 = then(m03, as_left(m45), m45)
    m46 = then(m45, lefts[6], maps[6])
    m06 = then(m03, as_left(m46), m46)
    for j, step_map in enumerate((maps[0], m01, m02, m03, m04, m05, m06)):
        prefix[j] = step_map.astype(BF16)
    build_outputs(2)

    loads[3].wait()
    first = jnp.concatenate([start_ref[...], jnp.zeros((HD, LANES - HD - 1), F32)], axis=1)
    entry = jnp.transpose(jnp.concatenate([jnp.zeros((HD, LANES), F32), first], axis=0))[:FEAT]
    for g in range(GROUPS - 1):
        @pl.when(g < group)
        def _(g=g):
            pltpu.make_async_remote_copy(
                src_ref=send2,
                dst_ref=recv2.at[g],
                send_sem=send_sem2.at[0],
                recv_sem=recv_sem2.at[g],
                device_id=(g * GROUP + place, head),
                device_id_type=MESH,
            ).wait_recv()

    half_pad = jnp.zeros((LANES - FEAT, LANES), BF16)

    def apply(left, step_map, old):
        padded = jnp.concatenate([old.astype(BF16), half_pad], axis=0)
        return old + jnp.where(lane_f < HD, 0.0, step_map) + dot(left, padded)

    passed = [
        unpack(jnp.where(g < group, recv2[g].astype(F32), 0.0)) for g in range(GROUPS - 1)
    ]
    for left, step_map in passed:
        entry = apply(left, step_map[:, :LANES], entry)

    def pack_state(rows):
        return jnp.concatenate(
            [
                jnp.where(lane[:32] < HD, pltpu.roll(rows[:32], HD, 1), rows[32:HD]),
                rows[HD:],
            ],
            axis=0,
        ).astype(BF16)

    send3[0] = pack_state(entry)
    for j in range(1, GROUP):
        before = prefix[j - 1].astype(F32)
        send3[j] = pack_state(apply(as_left(before), before[:, :LANES], entry))

    def back(step):
        peer = lax.rem(place + step, GROUP)
        return pltpu.make_async_remote_copy(
            src_ref=send3.at[peer],
            dst_ref=recv3.at[place],
            send_sem=send_sem3.at[step - 1],
            recv_sem=recv_sem3.at[place],
            device_id=(base + peer, head),
            device_id_type=MESH,
        )

    for step in (4, 5, 3, 2, 6, 7, 1):
        copy = back(step)
        copy.start()
        copies.append(copy)
    recv3[place] = send3[place]

    build_outputs(3)

    for step in range(1, GROUP):
        source = lax.rem(place + step, GROUP)
        pltpu.make_async_remote_copy(
            src_ref=send3.at[0],
            dst_ref=recv3.at[source],
            send_sem=send_sem3.at[0],
            recv_sem=recv_sem3.at[source],
            device_id=(base + source, head),
            device_id_type=MESH,
        ).wait_recv()
    loads[4].wait()

    def unpack_state(h):
        wide = recv3[h].astype(F32)
        turned = pltpu.roll(wide, HD, 1)
        odd = h % 2
        ours = (lane[: PACKED] < HD) != (odd == 1)
        same = jnp.where(ours, wide, 0.0)
        other = jnp.where(ours, turned, 0.0)
        if odd:
            parts = [other[:32], same[:32], same[32:]]
        else:
            parts = [same[:32], other[:32], other[32:]]
        return jnp.concatenate([jnp.concatenate(parts, axis=0).astype(BF16), rest], axis=0)

    states = [
        jnp.concatenate([unpack_state(2 * p), unpack_state(2 * p + 1)], axis=0)
        for p in range(PAIRS)
    ]

    def outputs_of(block):
        rows = pl.ds(pl.multiple_of(block * ROWS, ROWS), ROWS)
        return jnp.concatenate(
            [
                (dot(qt_ref[p, rows, :], states[p]) + py_ref[p, rows, :]).astype(BF16)
                for p in range(PAIRS)
            ],
            axis=1,
        )

    half = WIDTH // 2

    def project(z, side, piece):
        at = side * half + piece * 512
        return dot(z, w_ref[:, at : at + 512])

    def send(source, target, send_at, recv_at, peer):
        copy = pltpu.make_async_remote_copy(
            src_ref=source, dst_ref=target, send_sem=send_at, recv_sem=recv_at,
            device_id=(seq, peer), device_id_type=MESH,
        )
        copy.start()
        return copy

    def arrived(target, recv_at, peer):
        pltpu.make_async_remote_copy(
            src_ref=target, dst_ref=target, send_sem=far_send_sem.at[0, 0], recv_sem=recv_at,
            device_id=(seq, peer), device_id_type=MESH,
        ).wait_recv()

    chunks = range(CHUNKS)

    def chunk_rows(chunk):
        return pl.ds(chunk * CHUNK, CHUNK)

    z = outputs_of(lax.rem(head + 2, RING))
    for side, peer in ((0, up), (1, down)):
        for piece in (0, 1):
            far_send[side, :, piece * 512 : (piece + 1) * 512] = project(z, side, piece).astype(BF16)
        for chunk in chunks:
            copies.append(
                send(
                    far_send.at[side, chunk_rows(chunk)], far_recv.at[side, chunk_rows(chunk)],
                    far_send_sem.at[side, chunk], far_recv_sem.at[side, chunk], peer,
                )
            )
    z_near = [outputs_of(up), outputs_of(down)]
    def send_near(way, side, peer):
        copies.append(
            send(
                near_send.at[way, side], near_recv.at[way, side],
                near_send_sem.at[way], near_recv_sem.at[way], peer,
            )
        )

    for way in (0, 1):
        side = 1 - way
        for piece in (0, 1):
            near_send[way, side, :, piece * 512 : (piece + 1) * 512] = project(
                z_near[way], side, piece
            ).astype(BF16)
        send_near(way, side, (up, down)[way])
    merged = [[project(z_near[way], way, piece) for piece in (0, 1)] for way in (0, 1)]
    for chunk in chunks:
        for way, peer, source in ((0, up, down), (1, down, up)):
            rows = chunk_rows(chunk)
            arrived(far_recv.at[way, rows], far_recv_sem.at[way, chunk], source)
            for piece in (0, 1):
                cols = slice(piece * 512, (piece + 1) * 512)
                near_send[way, way, rows, cols] = (
                    merged[way][piece][chunk * CHUNK : (chunk + 1) * CHUNK]
                    + far_recv[way, rows, cols].astype(F32)
                ).astype(BF16)
            copies.append(
                send(
                    near_send.at[way, way, rows], near_recv.at[way, way, rows],
                    merge_send_sem.at[way, chunk], merge_recv_sem.at[way, chunk], peer,
                )
            )
    z = outputs_of(head)
    own = [[project(z, side, piece) for piece in (0, 1)] for side in (0, 1)]
    sources = (down, up)
    for way in (0, 1):
        arrived(near_recv.at[way, 1 - way], near_recv_sem.at[way], sources[way])
    for side in (0, 1):
        for piece in (0, 1):
            own[side][piece] = own[side][piece] + near_recv[
                1 - side, side, :, piece * 512 : (piece + 1) * 512
            ].astype(F32)
    for chunk in chunks:
        rows = chunk_rows(chunk)
        for side in (0, 1):
            arrived(near_recv.at[side, side, rows], merge_recv_sem.at[side, chunk], sources[side])
            for piece in (0, 1):
                at = side * half + piece * 512
                out_ref[rows, at : at + 512] = (
                    own[side][piece][chunk * CHUNK : (chunk + 1) * CHUNK]
                    + near_recv[side, side, rows, piece * 512 : (piece + 1) * 512].astype(F32)
                ).astype(BF16)

    for copy in copies:
        copy.wait_send()
    for step in range(1, GROUPS):
        @pl.when(group + step < GROUPS)
        def _(step=step):
            to_groups(step).wait_send()


def per_device(queries, keys, values, rates, start_state, out_weight):
    hbm = pl.BlockSpec(memory_space=pl.ANY)
    vmem = pl.BlockSpec(memory_space=pltpu.VMEM)
    dma = pltpu.SemaphoreType.DMA
    half = WIDTH // 2
    return pl.pallas_call(
        kernel,
        out_shape=jax.ShapeDtypeStruct((ROWS, WIDTH), BF16),
        in_specs=[hbm] * 6,
        out_specs=vmem,
        scratch_shapes=[
            pltpu.VMEM((TOK, 8 * HD), BF16),
            pltpu.VMEM((TOK, 8 * HD), BF16),
            pltpu.VMEM((TOK, 8 * HD), BF16),
            pltpu.VMEM((8 * HD, WIDTH), BF16),
            pltpu.VMEM((HD, HD + 1), F32),
            pltpu.VMEM((2 * PAIRS, TOK), F32),
            pltpu.VMEM((2 * PAIRS, TOK, 2 * LANES), BF16),
            pltpu.VMEM((2 * PAIRS, LANES, TOK), BF16),
            pltpu.VMEM((PAIRS, TOK, 2 * LANES), BF16),
            pltpu.VMEM((PAIRS, TOK, LANES), F32),
            pltpu.VMEM((PAIRS, 2, FEAT, LANES), BF16),
            pltpu.VMEM((GROUP, FEAT, LANES), BF16),
            pltpu.VMEM((GROUP - 1, FEAT, 2 * LANES), BF16),
            pltpu.VMEM((FEAT, LANES), BF16),
            pltpu.VMEM((GROUPS, FEAT, LANES), BF16),
            pltpu.VMEM((GROUP, PACKED, LANES), BF16),
            pltpu.VMEM((GROUP, PACKED, LANES), BF16),
            pltpu.VMEM((2, ROWS, half), BF16),
            pltpu.VMEM((2, ROWS, half), BF16),
            pltpu.VMEM((2, 2, ROWS, half), BF16),
            pltpu.VMEM((2, 2, ROWS, half), BF16),
            dma((6,)),
            dma((PAIRS, 2)),
            dma((GROUP,)),
            dma((GROUPS - 1,)),
            dma((GROUPS,)),
            dma((GROUP - 1,)),
            dma((GROUP,)),
            dma((2, CHUNKS)),
            dma((2, CHUNKS)),
            dma((2,)),
            dma((2,)),
            dma((2, CHUNKS)),
            dma((2, CHUNKS)),
        ],
        compiler_params=pltpu.CompilerParams(
            collective_id=0, has_side_effects=True, vmem_limit_bytes=54784 * 1024
        ),
    )(queries, keys, values, jnp.transpose(rates), start_state, out_weight)


def solution(mesh):
    in_specs = (
        P("seq", "head"),
        P("seq", "head"),
        P("seq", "head"),
        P("seq", "head"),
        P("head", None, None),
        P("head", None),
    )
    out_specs = P(("seq", "head"), None)
    return jax.shard_map(
        per_device, mesh=mesh, in_specs=in_specs, out_specs=out_specs, check_vma=False
    )
```

```python
import jax
import jax.numpy as jnp
from jax import lax
from jax.experimental import pallas as pl
from jax.experimental.pallas import tpu as pltpu
from jax.sharding import PartitionSpec as P

HD = 64
MINIBATCH_TOKENS = 16
TOK = 256
HALF = TOK // 2
PAIRS = 4
GROUP = 8
GROUPS = 4
RING = 4
FEAT = 80
LANES = 128
PACKED = 48
WIDTH = 2048
ROWS = TOK // RING
CHUNKS = 1
CHUNK = ROWS // CHUNKS
MESH = pl.DeviceIdType.MESH
F32 = jnp.float32
BF16 = jnp.bfloat16


def dot(left, right):
    return jnp.dot(left, right, preferred_element_type=F32)


def dot_t(left, right):
    return lax.dot_general(left, right, (((1,), (1,)), ((), ())), preferred_element_type=F32)


def kernel(
    q_hbm, k_hbm, v_hbm, rate_hbm, start_hbm, w_hbm, out_ref,
    q_ref, k_ref, v_ref, w_ref, start_ref, rate_ref,
    u_ref, kt_ref, qt_ref, py_ref,
    send1, recv1, prefix, send2, recv2, send3, recv3,
    far_send, far_recv, near_send, near_recv,
    load_sem, send_sem1, recv_sem1, send_sem2, recv_sem2, send_sem3, recv_sem3,
    far_send_sem, far_recv_sem, near_send_sem, near_recv_sem, merge_send_sem, merge_recv_sem,
):
    seq = lax.axis_index("seq")
    head = lax.axis_index("head")
    group = seq // GROUP
    place = lax.rem(seq, GROUP)
    chip = place // 2
    core = lax.rem(place, 2)
    base = group * GROUP

    loads = [
        pltpu.make_async_copy(k_hbm, k_ref, load_sem.at[0]),
        pltpu.make_async_copy(v_hbm, v_ref, load_sem.at[1]),
        pltpu.make_async_copy(q_hbm, q_ref, load_sem.at[2]),
        pltpu.make_async_copy(start_hbm.at[place], start_ref, load_sem.at[3]),
        pltpu.make_async_copy(w_hbm, w_ref, load_sem.at[4]),
        pltpu.make_async_copy(rate_hbm, rate_ref, load_sem.at[5]),
    ]
    for load in (loads[5], loads[0], loads[1]):
        load.start()

    barrier = pltpu.get_barrier_semaphore()
    for step in range(1, GROUP):
        pl.semaphore_signal(
            barrier, inc=1, device_id=(base + lax.rem(place + step, GROUP), head), device_id_type=MESH
        )
    for step in range(1, GROUPS):
        pl.semaphore_signal(
            barrier, inc=1,
            device_id=(lax.rem(group + step, GROUPS) * GROUP + place, head), device_id_type=MESH,
        )
    up = lax.rem(head + 1, RING)
    down = lax.rem(head + RING - 1, RING)
    for peer in (up, down):
        pl.semaphore_signal(barrier, inc=1, device_id=(seq, peer), device_id_type=MESH)

    lane = lax.broadcasted_iota(jnp.int32, (TOK, LANES), 1)
    is_one = jnp.where(lane == HD, 1.0, 0.0).astype(F32)
    row_h = lax.broadcasted_iota(jnp.int32, (HALF, HALF), 0)
    col_h = lax.broadcasted_iota(jnp.int32, (HALF, HALF), 1)
    earlier_block = row_h // MINIBATCH_TOKENS > col_h // MINIBATCH_TOKENS
    same_chunk = row_h // HD == col_h // HD
    near_mask = jnp.logical_and(earlier_block, same_chunk)
    far_mask = jnp.logical_and(earlier_block, jnp.logical_not(same_chunk))
    causal = row_h >= col_h

    one_b = is_one.astype(BF16)
    lane_f = lane[:FEAT]
    row_f = lax.broadcasted_iota(jnp.int32, (FEAT, LANES), 0)
    sign = jnp.where(lane_f < HD, -1.0, 1.0).astype(F32)
    lane_t = lane[:16]
    row_t = lax.broadcasted_iota(jnp.int32, (16, LANES), 0)
    pick = jnp.where(jnp.logical_and(row_t == 1, lane_t == HD), 1.0, 0.0).astype(BF16)
    diagonal = jnp.where(row_f == lane_f, 1.0, 0.0).astype(BF16)
    rest = jnp.zeros((LANES - FEAT, LANES), BF16)

    def pack(wide, column):
        in_row = dot_t(pick, jnp.concatenate([column.astype(BF16), rest], axis=0))
        return jnp.concatenate([wide[:HD], wide[HD:] + in_row], axis=0).astype(BF16)

    def unpack(packed):
        wide = packed.astype(F32)
        in_row = jnp.where(row_t == 0, pltpu.roll(wide[HD:], 15, 0), 0.0).astype(BF16)
        column = dot_t(
            diagonal, jnp.concatenate([jnp.zeros((HD, LANES), BF16), in_row, rest], axis=0)
        )
        wide = jnp.where(row_f <= HD, wide, 0.0)
        return (
            jnp.where(lane_f < HD, wide, column).astype(BF16),
            jnp.concatenate([wide, column], axis=1),
        )

    def with_one(pair, odd):
        wide = pair.astype(F32)
        if odd:
            wide = pltpu.roll(wide, HD, 1)
        return jnp.where(lane < HD, wide, is_one)

    def build_maps(slots, pairs):
        heads = [(i, e) for i in range(len(pairs)) for e in (0, 1)]
        at = {h: 2 * pairs[h[0]] + h[1] for h in heads}
        cols = [pl.ds(pl.multiple_of(p * LANES, LANES), LANES) for p in pairs]
        kp = [k_ref[:, c] for c in cols]
        vp = [v_ref[:, c].astype(F32) for c in cols]
        vf = {h: vp[h[0]] if h[1] else pltpu.roll(vp[h[0]], HD, 1) for h in heads}
        kf = {h: with_one(kp[h[0]], h[1]) for h in heads}
        kx = {h: kf[h].astype(BF16) for h in heads}
        ktf = {h: jnp.transpose(kf[h]) for h in heads}
        kt = {h: ktf[h].astype(BF16) for h in heads}
        rate = {h: rate_ref[pl.ds(at[h], 1), :] for h in heads}
        x = {
            h: jnp.concatenate([jnp.where(lane < HD, kf[h], vf[h]).astype(BF16), one_b], axis=1)
            for h in heads
        }
        low = {h: dot(kx[h], kt[h]) * rate[h] for h in heads}
        lows = {h: (low[h][:HALF, :HALF], low[h][HALF:, HALF:]) for h in heads}
        cross = {h: low[h][HALF:, :HALF].astype(BF16) for h in heads}
        both = [(h, b) for h in heads for b in (0, 1)]
        near = {hb: jnp.where(near_mask, lows[hb[0]][hb[1]], 0.0) for hb in both}
        far = {hb: jnp.where(far_mask, lows[hb[0]][hb[1]], 0.0) for hb in both}
        near_b = {hb: near[hb].astype(BF16) for hb in both}
        sq = {hb: dot(near_b[hb], near_b[hb]) for hb in both}
        n64 = {hb: sq[hb] - near[hb] - dot(near_b[hb], sq[hb].astype(BF16)) for hb in both}
        n64_b = {hb: n64[hb].astype(BF16) for hb in both}
        z = {hb: far[hb] + dot(n64_b[hb], far[hb].astype(BF16)) for hb in both}
        inv = {
            hb: (n64[hb] - z[hb] - dot(z[hb].astype(BF16), n64_b[hb])).astype(BF16) for hb in both
        }
        x0 = {h: x[h][:HALF] for h in heads}
        u0 = {h: (x0[h].astype(F32) + dot(inv[h, 0], x0[h])).astype(BF16) for h in heads}
        x1 = {h: x[h][HALF:].astype(F32) - dot(cross[h], u0[h]) for h in heads}
        u1 = {h: (x1[h] + dot(inv[h, 1], x1[h].astype(BF16))).astype(BF16) for h in heads}
        u = {h: jnp.concatenate([u0[h], u1[h]], axis=0) for h in heads}
        krt = {h: (ktf[h][:FEAT] * rate[h]).astype(BF16) for h in heads}
        maps = {h: dot(krt[h], u[h]) for h in heads}
        for h in heads:
            send1[slots[h[0]], h[1]] = pack(maps[h][:, :LANES] * sign, -maps[h][:, LANES:])
        for h in heads:
            u_ref[at[h]] = u[h]
            kt_ref[at[h]] = kt[h]

    def build_outputs(p):
        qp = q_ref[:, p * LANES : (p + 1) * LANES]
        for e in (0, 1):
            qf = with_one(qp, e)
            scores = dot(qf.astype(BF16), kt_ref[2 * p + e]) * rate_ref[2 * p + e : 2 * p + e + 1, :]
            top = jnp.where(causal, scores[:HALF, :HALF], 0.0).astype(BF16)
            last = jnp.where(causal, scores[HALF:, HALF:], 0.0).astype(BF16)
            bottom = jnp.concatenate([scores[HALF:, :HALF].astype(BF16), last], axis=1)
            pu = jnp.concatenate(
                [dot(top, u_ref[2 * p + e, :HALF, :]), dot(bottom, u_ref[2 * p + e])], axis=0
            )
            qt_ref[p, :, e * LANES : (e + 1) * LANES] = jnp.where(
                lane < HD, qf - pu[:, :LANES], is_one - pu[:, LANES:]
            ).astype(BF16)
            if e == 0:
                total = pltpu.roll(pu[:, :LANES], HD, 1)
            else:
                py_ref[p] = jnp.where(lane < HD, total, pu[:, :LANES])

    def to_group(slot, e, peer):
        return pltpu.make_async_remote_copy(
            src_ref=send1.at[slot, e],
            dst_ref=recv1.at[place],
            send_sem=send_sem1.at[slot, e],
            recv_sem=recv_sem1.at[place],
            device_id=(base + peer, head),
            device_id_type=MESH,
        )

    copies = []
    for load in (loads[5], loads[0], loads[1]):
        load.wait()
    for load in loads[2:5]:
        load.start()
    steps = (2, 3, 1, 0)
    for batch in ((0, 1), (2, 3)):
        pairs = [lax.rem(chip + steps[slot], PAIRS) for slot in batch]
        build_maps(batch, pairs)
        if batch[0] == 0:
            pl.semaphore_wait(barrier, GROUP - 1 + GROUPS - 1 + 2)
        for slot, p in zip(batch, pairs):
            if steps[slot]:
                for e in (0, 1):
                    copy = to_group(slot, e, 2 * p + e)
                    copy.start()
                    copies.append(copy)
            else:
                copy = to_group(slot, 1 - core, 2 * p + 1 - core)
                copy.start()
                copies.append(copy)
                recv1[place] = send1[slot, core]

    loads[2].wait()
    build_outputs(0)
    build_outputs(1)

    pad = jnp.zeros((LANES - FEAT, 2 * LANES), BF16)
    for j in range(GROUP):
        @pl.when(place != j)
        def _(j=j):
            pltpu.make_async_remote_copy(
                src_ref=send1.at[0, 0],
                dst_ref=recv1.at[j],
                send_sem=send_sem1.at[0, 0],
                recv_sem=recv_sem1.at[j],
                device_id=(base + j, head),
                device_id_type=MESH,
            ).wait_recv()

    def as_left(step_map):
        return jnp.where(lane_f < HD, step_map[:, :LANES], step_map[:, LANES:]).astype(BF16)

    def then(earlier, left, later):
        padded = jnp.concatenate([earlier.astype(BF16), pad], axis=0)
        return earlier + later + dot(left, padded)

    lefts, maps = zip(*[unpack(recv1[j]) for j in range(GROUP)])
    m01, m23, m45, m67 = [then(maps[j], lefts[j + 1], maps[j + 1]) for j in (0, 2, 4, 6)]
    m03 = then(m01, as_left(m23), m23)
    m47 = then(m45, as_left(m67), m67)
    m07 = then(m03, as_left(m47), m47)
    send2[...] = pack(m07[:, :LANES], m07[:, LANES:])

    def to_groups(step):
        return pltpu.make_async_remote_copy(
            src_ref=send2,
            dst_ref=recv2.at[group],
            send_sem=send_sem2.at[step - 1],
            recv_sem=recv_sem2.at[group],
            device_id=((group + step) * GROUP + place, head),
            device_id_type=MESH,
        )

    for step in range(1, GROUPS):
        @pl.when(group + step < GROUPS)
        def _(step=step):
            to_groups(step).start()

    m02 = then(m01, lefts[2], maps[2])
    m04 = then(m03, lefts[4], maps[4])
    m05 = then(m03, as_left(m45), m45)
    m46 = then(m45, lefts[6], maps[6])
    m06 = then(m03, as_left(m46), m46)
    for j, step_map in enumerate((maps[0], m01, m02, m03, m04, m05, m06)):
        prefix[j] = step_map.astype(BF16)
    build_outputs(2)

    loads[3].wait()
    first = jnp.concatenate([start_ref[...], jnp.zeros((HD, LANES - HD - 1), F32)], axis=1)
    entry = jnp.transpose(jnp.concatenate([jnp.zeros((HD, LANES), F32), first], axis=0))[:FEAT]
    for g in range(GROUPS - 1):
        @pl.when(g < group)
        def _(g=g):
            pltpu.make_async_remote_copy(
                src_ref=send2,
                dst_ref=recv2.at[g],
                send_sem=send_sem2.at[0],
                recv_sem=recv_sem2.at[g],
                device_id=(g * GROUP + place, head),
                device_id_type=MESH,
            ).wait_recv()

    half_pad = jnp.zeros((LANES - FEAT, LANES), BF16)

    def apply(left, step_map, old):
        padded = jnp.concatenate([old.astype(BF16), half_pad], axis=0)
        return old + jnp.where(lane_f < HD, 0.0, step_map) + dot(left, padded)

    passed = [
        unpack(jnp.where(g < group, recv2[g].astype(F32), 0.0)) for g in range(GROUPS - 1)
    ]
    for left, step_map in passed:
        entry = apply(left, step_map[:, :LANES], entry)

    def pack_state(rows):
        return jnp.concatenate(
            [
                jnp.where(lane[:32] < HD, pltpu.roll(rows[:32], HD, 1), rows[32:HD]),
                rows[HD:],
            ],
            axis=0,
        ).astype(BF16)

    send3[0] = pack_state(entry)
    for j in range(1, GROUP):
        before = prefix[j - 1].astype(F32)
        send3[j] = pack_state(apply(as_left(before), before[:, :LANES], entry))

    def back(step):
        peer = lax.rem(place + step, GROUP)
        return pltpu.make_async_remote_copy(
            src_ref=send3.at[peer],
            dst_ref=recv3.at[place],
            send_sem=send_sem3.at[step - 1],
            recv_sem=recv_sem3.at[place],
            device_id=(base + peer, head),
            device_id_type=MESH,
        )

    for step in (4, 5, 3, 2, 6, 7, 1):
        copy = back(step)
        copy.start()
        copies.append(copy)
    recv3[place] = send3[place]

    build_outputs(3)

    for step in range(1, GROUP):
        source = lax.rem(place + step, GROUP)
        pltpu.make_async_remote_copy(
            src_ref=send3.at[0],
            dst_ref=recv3.at[source],
            send_sem=send_sem3.at[0],
            recv_sem=recv_sem3.at[source],
            device_id=(base + source, head),
            device_id_type=MESH,
        ).wait_recv()
    loads[4].wait()

    def unpack_state(h):
        wide = recv3[h].astype(F32)
        turned = pltpu.roll(wide, HD, 1)
        odd = h % 2
        ours = (lane[: PACKED] < HD) != (odd == 1)
        same = jnp.where(ours, wide, 0.0)
        other = jnp.where(ours, turned, 0.0)
        if odd:
            parts = [other[:32], same[:32], same[32:]]
        else:
            parts = [same[:32], other[:32], other[32:]]
        return jnp.concatenate([jnp.concatenate(parts, axis=0).astype(BF16), rest], axis=0)

    states = [
        jnp.concatenate([unpack_state(2 * p), unpack_state(2 * p + 1)], axis=0)
        for p in range(PAIRS)
    ]

    def outputs_of(block):
        rows = pl.ds(pl.multiple_of(block * ROWS, ROWS), ROWS)
        return jnp.concatenate(
            [
                (dot(qt_ref[p, rows, :], states[p]) + py_ref[p, rows, :]).astype(BF16)
                for p in range(PAIRS)
            ],
            axis=1,
        )

    half = WIDTH // 2

    def project(z, side, piece):
        at = side * half + piece * 512
        return dot(z, w_ref[:, at : at + 512])

    def send(source, target, send_at, recv_at, peer):
        copy = pltpu.make_async_remote_copy(
            src_ref=source, dst_ref=target, send_sem=send_at, recv_sem=recv_at,
            device_id=(seq, peer), device_id_type=MESH,
        )
        copy.start()
        return copy

    def arrived(target, recv_at, peer):
        pltpu.make_async_remote_copy(
            src_ref=target, dst_ref=target, send_sem=far_send_sem.at[0, 0], recv_sem=recv_at,
            device_id=(seq, peer), device_id_type=MESH,
        ).wait_recv()

    chunks = range(CHUNKS)

    def chunk_rows(chunk):
        return pl.ds(chunk * CHUNK, CHUNK)

    z = outputs_of(lax.rem(head + 2, RING))
    for side, peer in ((0, up), (1, down)):
        for piece in (0, 1):
            far_send[side, :, piece * 512 : (piece + 1) * 512] = project(z, side, piece).astype(BF16)
        for chunk in chunks:
            copies.append(
                send(
                    far_send.at[side, chunk_rows(chunk)], far_recv.at[side, chunk_rows(chunk)],
                    far_send_sem.at[side, chunk], far_recv_sem.at[side, chunk], peer,
                )
            )
    z_near = [outputs_of(up), outputs_of(down)]
    def send_near(way, side, peer):
        copies.append(
            send(
                near_send.at[way, side], near_recv.at[way, side],
                near_send_sem.at[way], near_recv_sem.at[way], peer,
            )
        )

    for way in (0, 1):
        side = 1 - way
        for piece in (0, 1):
            near_send[way, side, :, piece * 512 : (piece + 1) * 512] = project(
                z_near[way], side, piece
            ).astype(BF16)
        send_near(way, side, (up, down)[way])
    merged = [[project(z_near[way], way, piece) for piece in (0, 1)] for way in (0, 1)]
    for chunk in chunks:
        for way, peer, source in ((0, up, down), (1, down, up)):
            rows = chunk_rows(chunk)
            arrived(far_recv.at[way, rows], far_recv_sem.at[way, chunk], source)
            for piece in (0, 1):
                cols = slice(piece * 512, (piece + 1) * 512)
                near_send[way, way, rows, cols] = (
                    merged[way][piece][chunk * CHUNK : (chunk + 1) * CHUNK]
                    + far_recv[way, rows, cols].astype(F32)
                ).astype(BF16)
            copies.append(
                send(
                    near_send.at[way, way, rows], near_recv.at[way, way, rows],
                    merge_send_sem.at[way, chunk], merge_recv_sem.at[way, chunk], peer,
                )
            )
    z = outputs_of(head)
    own = [[project(z, side, piece) for piece in (0, 1)] for side in (0, 1)]
    sources = (down, up)
    for way in (0, 1):
        arrived(near_recv.at[way, 1 - way], near_recv_sem.at[way], sources[way])
    for side in (0, 1):
        for piece in (0, 1):
            own[side][piece] = own[side][piece] + near_recv[
                1 - side, side, :, piece * 512 : (piece + 1) * 512
            ].astype(F32)
    for chunk in chunks:
        rows = chunk_rows(chunk)
        for side in (0, 1):
            arrived(near_recv.at[side, side, rows], merge_recv_sem.at[side, chunk], sources[side])
            for piece in (0, 1):
                at = side * half + piece * 512
                out_ref[rows, at : at + 512] = (
                    own[side][piece][chunk * CHUNK : (chunk + 1) * CHUNK]
                    + near_recv[side, side, rows, piece * 512 : (piece + 1) * 512].astype(F32)
                ).astype(BF16)

    for copy in copies:
        copy.wait_send()
    for step in range(1, GROUPS):
        @pl.when(group + step < GROUPS)
        def _(step=step):
            to_groups(step).wait_send()


def per_device(queries, keys, values, rates, start_state, out_weight):
    hbm = pl.BlockSpec(memory_space=pl.ANY)
    vmem = pl.BlockSpec(memory_space=pltpu.VMEM)
    dma = pltpu.SemaphoreType.DMA
    half = WIDTH // 2
    return pl.pallas_call(
        kernel,
        out_shape=jax.ShapeDtypeStruct((ROWS, WIDTH), BF16),
        in_specs=[hbm] * 6,
        out_specs=vmem,
        scratch_shapes=[
            pltpu.VMEM((TOK, 8 * HD), BF16),
            pltpu.VMEM((TOK, 8 * HD), BF16),
            pltpu.VMEM((TOK, 8 * HD), BF16),
            pltpu.VMEM((8 * HD, WIDTH), BF16),
            pltpu.VMEM((HD, HD + 1), F32),
            pltpu.VMEM((2 * PAIRS, TOK), F32),
            pltpu.VMEM((2 * PAIRS, TOK, 2 * LANES), BF16),
            pltpu.VMEM((2 * PAIRS, LANES, TOK), BF16),
            pltpu.VMEM((PAIRS, TOK, 2 * LANES), BF16),
            pltpu.VMEM((PAIRS, TOK, LANES), F32),
            pltpu.VMEM((PAIRS, 2, FEAT, LANES), BF16),
            pltpu.VMEM((GROUP, FEAT, LANES), BF16),
            pltpu.VMEM((GROUP - 1, FEAT, 2 * LANES), BF16),
            pltpu.VMEM((FEAT, LANES), BF16),
            pltpu.VMEM((GROUPS, FEAT, LANES), BF16),
            pltpu.VMEM((GROUP, PACKED, LANES), BF16),
            pltpu.VMEM((GROUP, PACKED, LANES), BF16),
            pltpu.VMEM((2, ROWS, half), BF16),
            pltpu.VMEM((2, ROWS, half), BF16),
            pltpu.VMEM((2, 2, ROWS, half), BF16),
            pltpu.VMEM((2, 2, ROWS, half), BF16),
            dma((6,)),
            dma((PAIRS, 2)),
            dma((GROUP,)),
            dma((GROUPS - 1,)),
            dma((GROUPS,)),
            dma((GROUP - 1,)),
            dma((GROUP,)),
            dma((2, CHUNKS)),
            dma((2, CHUNKS)),
            dma((2,)),
            dma((2,)),
            dma((2, CHUNKS)),
            dma((2, CHUNKS)),
        ],
        compiler_params=pltpu.CompilerParams(
            collective_id=0, has_side_effects=True, vmem_limit_bytes=54784 * 1024
        ),
    )(queries, keys, values, jnp.transpose(rates), start_state, out_weight)


def solution(mesh):
    in_specs = (
        P("seq", "head"),
        P("seq", "head"),
        P("seq", "head"),
        P("seq", "head"),
        P("head", None, None),
        P("head", None),
    )
    out_specs = P(("seq", "head"), None)
    return jax.shard_map(
        per_device, mesh=mesh, in_specs=in_specs, out_specs=out_specs, check_vma=False
    )
```

```python
import jax
import jax.numpy as jnp
from jax import lax
from jax.experimental import pallas as pl
from jax.experimental.pallas import tpu as pltpu
from jax.sharding import PartitionSpec as P

HD = 64
MINIBATCH_TOKENS = 16
TOK = 256
HALF = TOK // 2
PAIRS = 4
GROUP = 8
GROUPS = 4
RING = 4
FEAT = 80
LANES = 128
PACKED = 48
WIDTH = 2048
ROWS = TOK // RING
CHUNKS = 1
CHUNK = ROWS // CHUNKS
MESH = pl.DeviceIdType.MESH
F32 = jnp.float32
BF16 = jnp.bfloat16


def dot(left, right):
    return jnp.dot(left, right, preferred_element_type=F32)


def dot_t(left, right):
    return lax.dot_general(left, right, (((1,), (1,)), ((), ())), preferred_element_type=F32)


def kernel(
    q_hbm, k_hbm, v_hbm, rate_hbm, start_hbm, w_hbm, out_ref,
    q_ref, k_ref, v_ref, w_ref, start_ref, rate_ref,
    u_ref, kt_ref, qt_ref, py_ref,
    send1, recv1, prefix, send2, recv2, send3, recv3,
    far_send, far_recv, near_send, near_recv,
    load_sem, send_sem1, recv_sem1, send_sem2, recv_sem2, send_sem3, recv_sem3,
    far_send_sem, far_recv_sem, near_send_sem, near_recv_sem, merge_send_sem, merge_recv_sem,
):
    seq = lax.axis_index("seq")
    head = lax.axis_index("head")
    group = seq // GROUP
    place = lax.rem(seq, GROUP)
    chip = place // 2
    core = lax.rem(place, 2)
    base = group * GROUP

    loads = [
        pltpu.make_async_copy(k_hbm, k_ref, load_sem.at[0]),
        pltpu.make_async_copy(v_hbm, v_ref, load_sem.at[1]),
        pltpu.make_async_copy(q_hbm, q_ref, load_sem.at[2]),
        pltpu.make_async_copy(start_hbm.at[place], start_ref, load_sem.at[3]),
        pltpu.make_async_copy(w_hbm, w_ref, load_sem.at[4]),
        pltpu.make_async_copy(rate_hbm, rate_ref, load_sem.at[5]),
    ]
    for load in (loads[5], loads[0], loads[1]):
        load.start()

    barrier = pltpu.get_barrier_semaphore()
    for step in range(1, GROUP):
        pl.semaphore_signal(
            barrier, inc=1, device_id=(base + lax.rem(place + step, GROUP), head), device_id_type=MESH
        )
    for step in range(1, GROUPS):
        pl.semaphore_signal(
            barrier, inc=1,
            device_id=(lax.rem(group + step, GROUPS) * GROUP + place, head), device_id_type=MESH,
        )
    up = lax.rem(head + 1, RING)
    down = lax.rem(head + RING - 1, RING)
    for peer in (up, down):
        pl.semaphore_signal(barrier, inc=1, device_id=(seq, peer), device_id_type=MESH)

    lane = lax.broadcasted_iota(jnp.int32, (TOK, LANES), 1)
    is_one = jnp.where(lane == HD, 1.0, 0.0).astype(F32)
    row_h = lax.broadcasted_iota(jnp.int32, (HALF, HALF), 0)
    col_h = lax.broadcasted_iota(jnp.int32, (HALF, HALF), 1)
    earlier_block = row_h // MINIBATCH_TOKENS > col_h // MINIBATCH_TOKENS
    same_chunk = row_h // HD == col_h // HD
    near_mask = jnp.logical_and(earlier_block, same_chunk)
    far_mask = jnp.logical_and(earlier_block, jnp.logical_not(same_chunk))
    causal = row_h >= col_h

    one_b = is_one.astype(BF16)
    lane_f = lane[:FEAT]
    row_f = lax.broadcasted_iota(jnp.int32, (FEAT, LANES), 0)
    sign = jnp.where(lane_f < HD, -1.0, 1.0).astype(F32)
    lane_t = lane[:16]
    row_t = lax.broadcasted_iota(jnp.int32, (16, LANES), 0)
    pick = jnp.where(jnp.logical_and(row_t == 1, lane_t == HD), 1.0, 0.0).astype(BF16)
    diagonal = jnp.where(row_f == lane_f, 1.0, 0.0).astype(BF16)
    rest = jnp.zeros((LANES - FEAT, LANES), BF16)

    def pack(wide, column):
        in_row = dot_t(pick, jnp.concatenate([column.astype(BF16), rest], axis=0))
        return jnp.concatenate([wide[:HD], wide[HD:] + in_row], axis=0).astype(BF16)

    def unpack(packed):
        wide = packed.astype(F32)
        in_row = jnp.where(row_t == 0, pltpu.roll(wide[HD:], 15, 0), 0.0).astype(BF16)
        column = dot_t(
            diagonal, jnp.concatenate([jnp.zeros((HD, LANES), BF16), in_row, rest], axis=0)
        )
        wide = jnp.where(row_f <= HD, wide, 0.0)
        return (
            jnp.where(lane_f < HD, wide, column).astype(BF16),
            jnp.concatenate([wide, column], axis=1),
        )

    def with_one(pair, odd):
        wide = pair.astype(F32)
        if odd:
            wide = pltpu.roll(wide, HD, 1)
        return jnp.where(lane < HD, wide, is_one)

    def build_maps(slots, pairs):
        heads = [(i, e) for i in range(len(pairs)) for e in (0, 1)]
        at = {h: 2 * pairs[h[0]] + h[1] for h in heads}
        cols = [pl.ds(pl.multiple_of(p * LANES, LANES), LANES) for p in pairs]
        kp = [k_ref[:, c] for c in cols]
        vp = [v_ref[:, c].astype(F32) for c in cols]
        vf = {h: vp[h[0]] if h[1] else pltpu.roll(vp[h[0]], HD, 1) for h in heads}
        kf = {h: with_one(kp[h[0]], h[1]) for h in heads}
        kx = {h: kf[h].astype(BF16) for h in heads}
        ktf = {h: jnp.transpose(kf[h]) for h in heads}
        kt = {h: ktf[h].astype(BF16) for h in heads}
        rate = {h: rate_ref[pl.ds(at[h], 1), :] for h in heads}
        x = {
            h: jnp.concatenate([jnp.where(lane < HD, kf[h], vf[h]).astype(BF16), one_b], axis=1)
            for h in heads
        }
        low = {h: dot(kx[h], kt[h]) * rate[h] for h in heads}
        lows = {h: (low[h][:HALF, :HALF], low[h][HALF:, HALF:]) for h in heads}
        cross = {h: low[h][HALF:, :HALF].astype(BF16) for h in heads}
        both = [(h, b) for h in heads for b in (0, 1)]
        near = {hb: jnp.where(near_mask, lows[hb[0]][hb[1]], 0.0) for hb in both}
        far = {hb: jnp.where(far_mask, lows[hb[0]][hb[1]], 0.0) for hb in both}
        near_b = {hb: near[hb].astype(BF16) for hb in both}
        sq = {hb: dot(near_b[hb], near_b[hb]) for hb in both}
        n64 = {hb: sq[hb] - near[hb] - dot(near_b[hb], sq[hb].astype(BF16)) for hb in both}
        n64_b = {hb: n64[hb].astype(BF16) for hb in both}
        z = {hb: far[hb] + dot(n64_b[hb], far[hb].astype(BF16)) for hb in both}
        inv = {
            hb: (n64[hb] - z[hb] - dot(z[hb].astype(BF16), n64_b[hb])).astype(BF16) for hb in both
        }
        x0 = {h: x[h][:HALF] for h in heads}
        u0 = {h: (x0[h].astype(F32) + dot(inv[h, 0], x0[h])).astype(BF16) for h in heads}
        x1 = {h: x[h][HALF:].astype(F32) - dot(cross[h], u0[h]) for h in heads}
        u1 = {h: (x1[h] + dot(inv[h, 1], x1[h].astype(BF16))).astype(BF16) for h in heads}
        u = {h: jnp.concatenate([u0[h], u1[h]], axis=0) for h in heads}
        krt = {h: (ktf[h][:FEAT] * rate[h]).astype(BF16) for h in heads}
        maps = {h: dot(krt[h], u[h]) for h in heads}
        for h in heads:
            send1[slots[h[0]], h[1]] = pack(maps[h][:, :LANES] * sign, -maps[h][:, LANES:])
        for h in heads:
            u_ref[at[h]] = u[h]
            kt_ref[at[h]] = kt[h]

    def build_outputs(p):
        qp = q_ref[:, p * LANES : (p + 1) * LANES]
        for e in (0, 1):
            qf = with_one(qp, e)
            scores = dot(qf.astype(BF16), kt_ref[2 * p + e]) * rate_ref[2 * p + e : 2 * p + e + 1, :]
            top = jnp.where(causal, scores[:HALF, :HALF], 0.0).astype(BF16)
            last = jnp.where(causal, scores[HALF:, HALF:], 0.0).astype(BF16)
            bottom = jnp.concatenate([scores[HALF:, :HALF].astype(BF16), last], axis=1)
            pu = jnp.concatenate(
                [dot(top, u_ref[2 * p + e, :HALF, :]), dot(bottom, u_ref[2 * p + e])], axis=0
            )
            qt_ref[p, :, e * LANES : (e + 1) * LANES] = jnp.where(
                lane < HD, qf - pu[:, :LANES], is_one - pu[:, LANES:]
            ).astype(BF16)
            if e == 0:
                total = pltpu.roll(pu[:, :LANES], HD, 1)
            else:
                py_ref[p] = jnp.where(lane < HD, total, pu[:, :LANES])

    def to_group(slot, e, peer):
        return pltpu.make_async_remote_copy(
            src_ref=send1.at[slot, e],
            dst_ref=recv1.at[place],
            send_sem=send_sem1.at[slot, e],
            recv_sem=recv_sem1.at[place],
            device_id=(base + peer, head),
            device_id_type=MESH,
        )

    copies = []
    for load in (loads[5], loads[0], loads[1]):
        load.wait()
    for load in loads[2:5]:
        load.start()
    steps = (2, 3, 1, 0)
    for batch in ((0, 1), (2, 3)):
        pairs = [lax.rem(chip + steps[slot], PAIRS) for slot in batch]
        build_maps(batch, pairs)
        if batch[0] == 0:
            pl.semaphore_wait(barrier, GROUP - 1 + GROUPS - 1 + 2)
        for slot, p in zip(batch, pairs):
            if steps[slot]:
                for e in (0, 1):
                    copy = to_group(slot, e, 2 * p + e)
                    copy.start()
                    copies.append(copy)
            else:
                copy = to_group(slot, 1 - core, 2 * p + 1 - core)
                copy.start()
                copies.append(copy)
                recv1[place] = send1[slot, core]

    loads[2].wait()
    build_outputs(0)
    build_outputs(1)

    pad = jnp.zeros((LANES - FEAT, 2 * LANES), BF16)
    for j in range(GROUP):
        @pl.when(place != j)
        def _(j=j):
            pltpu.make_async_remote_copy(
                src_ref=send1.at[0, 0],
                dst_ref=recv1.at[j],
                send_sem=send_sem1.at[0, 0],
                recv_sem=recv_sem1.at[j],
                device_id=(base + j, head),
                device_id_type=MESH,
            ).wait_recv()

    def as_left(step_map):
        return jnp.where(lane_f < HD, step_map[:, :LANES], step_map[:, LANES:]).astype(BF16)

    def then(earlier, left, later):
        padded = jnp.concatenate([earlier.astype(BF16), pad], axis=0)
        return earlier + later + dot(left, padded)

    lefts, maps = zip(*[unpack(recv1[j]) for j in range(GROUP)])
    m01, m23, m45, m67 = [then(maps[j], lefts[j + 1], maps[j + 1]) for j in (0, 2, 4, 6)]
    m03 = then(m01, as_left(m23), m23)
    m47 = then(m45, as_left(m67), m67)
    m07 = then(m03, as_left(m47), m47)
    send2[...] = pack(m07[:, :LANES], m07[:, LANES:])

    def to_groups(step):
        return pltpu.make_async_remote_copy(
            src_ref=send2,
            dst_ref=recv2.at[group],
            send_sem=send_sem2.at[step - 1],
            recv_sem=recv_sem2.at[group],
            device_id=((group + step) * GROUP + place, head),
            device_id_type=MESH,
        )

    for step in (3, 2, 1):
        @pl.when(group + step < GROUPS)
        def _(step=step):
            to_groups(step).start()

    m02 = then(m01, lefts[2], maps[2])
    m04 = then(m03, lefts[4], maps[4])
    m05 = then(m03, as_left(m45), m45)
    m46 = then(m45, lefts[6], maps[6])
    m06 = then(m03, as_left(m46), m46)
    for j, step_map in enumerate((maps[0], m01, m02, m03, m04, m05, m06)):
        prefix[j] = step_map.astype(BF16)
    build_outputs(2)

    loads[3].wait()
    first = jnp.concatenate([start_ref[...], jnp.zeros((HD, LANES - HD - 1), F32)], axis=1)
    entry = jnp.transpose(jnp.concatenate([jnp.zeros((HD, LANES), F32), first], axis=0))[:FEAT]
    for g in range(GROUPS - 1):
        @pl.when(g < group)
        def _(g=g):
            pltpu.make_async_remote_copy(
                src_ref=send2,
                dst_ref=recv2.at[g],
                send_sem=send_sem2.at[0],
                recv_sem=recv_sem2.at[g],
                device_id=(g * GROUP + place, head),
                device_id_type=MESH,
            ).wait_recv()

    half_pad = jnp.zeros((LANES - FEAT, LANES), BF16)

    def apply(left, step_map, old):
        padded = jnp.concatenate([old.astype(BF16), half_pad], axis=0)
        return old + jnp.where(lane_f < HD, 0.0, step_map) + dot(left, padded)

    passed = [
        unpack(jnp.where(g < group, recv2[g].astype(F32), 0.0)) for g in range(GROUPS - 1)
    ]
    for left, step_map in passed:
        entry = apply(left, step_map[:, :LANES], entry)

    def pack_state(rows):
        return jnp.concatenate(
            [
                jnp.where(lane[:32] < HD, pltpu.roll(rows[:32], HD, 1), rows[32:HD]),
                rows[HD:],
            ],
            axis=0,
        ).astype(BF16)

    send3[0] = pack_state(entry)
    for j in range(1, GROUP):
        before = prefix[j - 1].astype(F32)
        send3[j] = pack_state(apply(as_left(before), before[:, :LANES], entry))

    def back(step):
        peer = lax.rem(place + step, GROUP)
        return pltpu.make_async_remote_copy(
            src_ref=send3.at[peer],
            dst_ref=recv3.at[place],
            send_sem=send_sem3.at[step - 1],
            recv_sem=recv_sem3.at[place],
            device_id=(base + peer, head),
            device_id_type=MESH,
        )

    for step in (4, 5, 3, 2, 6, 7, 1):
        copy = back(step)
        copy.start()
        copies.append(copy)
    recv3[place] = send3[place]

    build_outputs(3)

    for step in range(1, GROUP):
        source = lax.rem(place + step, GROUP)
        pltpu.make_async_remote_copy(
            src_ref=send3.at[0],
            dst_ref=recv3.at[source],
            send_sem=send_sem3.at[0],
            recv_sem=recv_sem3.at[source],
            device_id=(base + source, head),
            device_id_type=MESH,
        ).wait_recv()
    loads[4].wait()

    def unpack_state(h):
        wide = recv3[h].astype(F32)
        turned = pltpu.roll(wide, HD, 1)
        odd = h % 2
        ours = (lane[: PACKED] < HD) != (odd == 1)
        same = jnp.where(ours, wide, 0.0)
        other = jnp.where(ours, turned, 0.0)
        if odd:
            parts = [other[:32], same[:32], same[32:]]
        else:
            parts = [same[:32], other[:32], other[32:]]
        return jnp.concatenate([jnp.concatenate(parts, axis=0).astype(BF16), rest], axis=0)

    states = [
        jnp.concatenate([unpack_state(2 * p), unpack_state(2 * p + 1)], axis=0)
        for p in range(PAIRS)
    ]

    def outputs_of(block):
        rows = pl.ds(pl.multiple_of(block * ROWS, ROWS), ROWS)
        return jnp.concatenate(
            [
                (dot(qt_ref[p, rows, :], states[p]) + py_ref[p, rows, :]).astype(BF16)
                for p in range(PAIRS)
            ],
            axis=1,
        )

    half = WIDTH // 2

    def project(z, side, piece):
        at = side * half + piece * 512
        return dot(z, w_ref[:, at : at + 512])

    def send(source, target, send_at, recv_at, peer):
        copy = pltpu.make_async_remote_copy(
            src_ref=source, dst_ref=target, send_sem=send_at, recv_sem=recv_at,
            device_id=(seq, peer), device_id_type=MESH,
        )
        copy.start()
        return copy

    def arrived(target, recv_at, peer):
        pltpu.make_async_remote_copy(
            src_ref=target, dst_ref=target, send_sem=far_send_sem.at[0, 0], recv_sem=recv_at,
            device_id=(seq, peer), device_id_type=MESH,
        ).wait_recv()

    chunks = range(CHUNKS)

    def chunk_rows(chunk):
        return pl.ds(chunk * CHUNK, CHUNK)

    z = outputs_of(lax.rem(head + 2, RING))
    for side, peer in ((0, up), (1, down)):
        for piece in (0, 1):
            far_send[side, :, piece * 512 : (piece + 1) * 512] = project(z, side, piece).astype(BF16)
        for chunk in chunks:
            copies.append(
                send(
                    far_send.at[side, chunk_rows(chunk)], far_recv.at[side, chunk_rows(chunk)],
                    far_send_sem.at[side, chunk], far_recv_sem.at[side, chunk], peer,
                )
            )
    z_near = [outputs_of(up), outputs_of(down)]
    def send_near(way, side, peer):
        copies.append(
            send(
                near_send.at[way, side], near_recv.at[way, side],
                near_send_sem.at[way], near_recv_sem.at[way], peer,
            )
        )

    for way in (0, 1):
        side = 1 - way
        for piece in (0, 1):
            near_send[way, side, :, piece * 512 : (piece + 1) * 512] = project(
                z_near[way], side, piece
            ).astype(BF16)
        send_near(way, side, (up, down)[way])
    merged = [[project(z_near[way], way, piece) for piece in (0, 1)] for way in (0, 1)]
    for chunk in chunks:
        for way, peer, source in ((0, up, down), (1, down, up)):
            rows = chunk_rows(chunk)
            arrived(far_recv.at[way, rows], far_recv_sem.at[way, chunk], source)
            for piece in (0, 1):
                cols = slice(piece * 512, (piece + 1) * 512)
                near_send[way, way, rows, cols] = (
                    merged[way][piece][chunk * CHUNK : (chunk + 1) * CHUNK]
                    + far_recv[way, rows, cols].astype(F32)
                ).astype(BF16)
            copies.append(
                send(
                    near_send.at[way, way, rows], near_recv.at[way, way, rows],
                    merge_send_sem.at[way, chunk], merge_recv_sem.at[way, chunk], peer,
                )
            )
    z = outputs_of(head)
    own = [[project(z, side, piece) for piece in (0, 1)] for side in (0, 1)]
    sources = (down, up)
    for way in (0, 1):
        arrived(near_recv.at[way, 1 - way], near_recv_sem.at[way], sources[way])
    for side in (0, 1):
        for piece in (0, 1):
            own[side][piece] = own[side][piece] + near_recv[
                1 - side, side, :, piece * 512 : (piece + 1) * 512
            ].astype(F32)
    for chunk in chunks:
        rows = chunk_rows(chunk)
        for side in (0, 1):
            arrived(near_recv.at[side, side, rows], merge_recv_sem.at[side, chunk], sources[side])
            for piece in (0, 1):
                at = side * half + piece * 512
                out_ref[rows, at : at + 512] = (
                    own[side][piece][chunk * CHUNK : (chunk + 1) * CHUNK]
                    + near_recv[side, side, rows, piece * 512 : (piece + 1) * 512].astype(F32)
                ).astype(BF16)

    for copy in copies:
        copy.wait_send()
    for step in range(1, GROUPS):
        @pl.when(group + step < GROUPS)
        def _(step=step):
            to_groups(step).wait_send()


def per_device(queries, keys, values, rates, start_state, out_weight):
    hbm = pl.BlockSpec(memory_space=pl.ANY)
    vmem = pl.BlockSpec(memory_space=pltpu.VMEM)
    dma = pltpu.SemaphoreType.DMA
    half = WIDTH // 2
    return pl.pallas_call(
        kernel,
        out_shape=jax.ShapeDtypeStruct((ROWS, WIDTH), BF16),
        in_specs=[hbm] * 6,
        out_specs=vmem,
        scratch_shapes=[
            pltpu.VMEM((TOK, 8 * HD), BF16),
            pltpu.VMEM((TOK, 8 * HD), BF16),
            pltpu.VMEM((TOK, 8 * HD), BF16),
            pltpu.VMEM((8 * HD, WIDTH), BF16),
            pltpu.VMEM((HD, HD + 1), F32),
            pltpu.VMEM((2 * PAIRS, TOK), F32),
            pltpu.VMEM((2 * PAIRS, TOK, 2 * LANES), BF16),
            pltpu.VMEM((2 * PAIRS, LANES, TOK), BF16),
            pltpu.VMEM((PAIRS, TOK, 2 * LANES), BF16),
            pltpu.VMEM((PAIRS, TOK, LANES), F32),
            pltpu.VMEM((PAIRS, 2, FEAT, LANES), BF16),
            pltpu.VMEM((GROUP, FEAT, LANES), BF16),
            pltpu.VMEM((GROUP - 1, FEAT, 2 * LANES), BF16),
            pltpu.VMEM((FEAT, LANES), BF16),
            pltpu.VMEM((GROUPS, FEAT, LANES), BF16),
            pltpu.VMEM((GROUP, PACKED, LANES), BF16),
            pltpu.VMEM((GROUP, PACKED, LANES), BF16),
            pltpu.VMEM((2, ROWS, half), BF16),
            pltpu.VMEM((2, ROWS, half), BF16),
            pltpu.VMEM((2, 2, ROWS, half), BF16),
            pltpu.VMEM((2, 2, ROWS, half), BF16),
            dma((6,)),
            dma((PAIRS, 2)),
            dma((GROUP,)),
            dma((GROUPS - 1,)),
            dma((GROUPS,)),
            dma((GROUP - 1,)),
            dma((GROUP,)),
            dma((2, CHUNKS)),
            dma((2, CHUNKS)),
            dma((2,)),
            dma((2,)),
            dma((2, CHUNKS)),
            dma((2, CHUNKS)),
        ],
        compiler_params=pltpu.CompilerParams(
            collective_id=0, has_side_effects=True, vmem_limit_bytes=54784 * 1024
        ),
    )(queries, keys, values, jnp.transpose(rates), start_state, out_weight)


def solution(mesh):
    in_specs = (
        P("seq", "head"),
        P("seq", "head"),
        P("seq", "head"),
        P("seq", "head"),
        P("head", None, None),
        P("head", None),
    )
    out_specs = P(("seq", "head"), None)
    return jax.shard_map(
        per_device, mesh=mesh, in_specs=in_specs, out_specs=out_specs, check_vma=False
    )
```
